32 devices in a mesh: ctx: 8 (over y, x, core), wsh: 4 (over z).
Axes of the slice: x: 2, y: 2, z: 4, core: 2. Of those that a mesh axis runs over, the one named last changes fastest.
Arguments:
- inputs: float32 [4, 1024, 2048], P('wsh', 'ctx'), may hold values from -6 to 6
- cotangent: float32 [4, 1024, 2048], P('wsh', 'ctx'), may hold values from -6 to 6
- block_order: int32 [4, 8], P('wsh'), may hold values from 0 to 7, each once within a row
- doc_cut: int32 [4], P('wsh'), may hold values from 256 to 768
- w_qkv: bfloat16 [2048, 6144], P(('ctx', 'wsh')), may hold values from -0.125 to 0.125
- b_qkv: bfloat16 [6144], P(('ctx', 'wsh')), may hold values from -3 to 3
- w_dense: bfloat16 [2048, 2048], P(('ctx', 'wsh')), may hold values from -0.75 to 0.75
- b_dense: bfloat16 [2048], P(('ctx', 'wsh')), may hold values from -4 to 4
- w_up: bfloat16 [2048, 8192], P(('ctx', 'wsh')), may hold values from -0.125 to 0.125
- b_up: bfloat16 [8192], P(('ctx', 'wsh')), may hold values from -3 to 3
- w_down: bfloat16 [8192, 2048], P(('ctx', 'wsh')), may hold values from -0.0625 to 0.0625
- b_down: bfloat16 [2048], P(('ctx', 'wsh')), may hold values from -4 to 4
- gain_attn: bfloat16 [2048], P(('ctx', 'wsh')), may hold values from 0.5 to 1.5
- shift_attn: bfloat16 [2048], P(('ctx', 'wsh')), may hold values from -3 to 3
- gain_mlp: bfloat16 [2048], P(('ctx', 'wsh')), may hold values from 0.099609375 to 1.8984375
- shift_mlp: bfloat16 [2048], P(('ctx', 'wsh')), may hold values from -3 to 3
Outputs:
- output: float32 [4, 1024, 2048], P('wsh', 'ctx')
- input_gradient: float32 [4, 1024, 2048], P('wsh', 'ctx')
- grad_w_qkv: float32 [2048, 6144], P(('ctx', 'wsh'))
- grad_b_qkv: float32 [6144], P(('ctx', 'wsh'))
- grad_w_dense: float32 [2048, 2048], P(('ctx', 'wsh'))
- grad_b_dense: float32 [2048], P(('ctx', 'wsh'))
- grad_w_up: float32 [2048, 8192], P(('ctx', 'wsh'))
- grad_b_up: float32 [8192], P(('ctx', 'wsh'))
- grad_w_down: float32 [8192, 2048], P(('ctx', 'wsh'))
- grad_b_down: float32 [2048], P(('ctx', 'wsh'))
- grad_gain_attn: float32 [2048], P(('ctx', 'wsh'))
- grad_shift_attn: float32 [2048], P(('ctx', 'wsh'))
- grad_gain_mlp: float32 [2048], P(('ctx', 'wsh'))
- grad_shift_mlp: float32 [2048], P(('ctx', 'wsh'))
The draws below stay inside these ranges and needn't reach their ends.
Inputs may be any that keep to these rules, and one draw needn't show every extreme that they name: Each row is a permutation; ctx index i holds, in its first and second 128/2 rows, blocks block_order[s, i] and 15 - block_order[s, i] of the sequence.
All inputs are finite; a program needn't handle non-finite values.
Results may differ from the reference program's by a relative error of at most 0.019.
Values may be sent and summed in bfloat16 or wider, within the bound.
No kernel may reach another device: no remote copies, remote signals or barrier semaphores. Data moves between devices by JAX's collectives and lax.ppermute only.
A program may use at most 512 MiB of HBM per device.

```python
import math
import jax
import jax.numpy as jnp
from jax import lax

D = 2048
HEADS = 8
HEAD_DIM = 256
ROT_DIM = 64
FF = 8192
TOK_DEV = 128
LENGTH = 1024
SEQS = 4
N_CTX = 8


def touch_ends(result, key, smallest, largest):
    dims = result.shape
    place = [jax.random.randint(jax.random.fold_in(key, axis), (), 0, dims[axis]) for axis in range(len(dims))]
    result = result.at[tuple(place)].set(smallest)
    longest = dims.index(max(dims))
    place[longest] = (place[longest] + 1) % dims[longest]
    return result.at[tuple(place)].set(largest)


def level_of(own_key, extent, pieces, low, top_value):
    def one(axis_at, blocks):
        draws = jax.random.uniform(jax.random.fold_in(jax.random.fold_in(own_key, 6), axis_at), (blocks,), jnp.float32, low / len(pieces), top_value / len(pieces))
        return jnp.repeat(jnp.exp(draws), extent[axis_at] // blocks).reshape((-1,) + (1,) * (len(extent) - axis_at - 1))

    gain = one(*pieces[0])
    for cut in pieces[1:]:
        gain = gain * one(*cut)
    return gain


def bell_draw(own_key, shape, spread, limit, split=(), held_as=jnp.bfloat16):
    drawn = jax.random.normal(own_key, shape, jnp.float32) * spread
    if len(split) > 0:
        drawn = level_of(own_key, shape, split, -0.22, 0.18) * drawn
    return jnp.clip(drawn, min=-limit, max=limit).astype(held_as)


def setup_inputs(seed: int = 0) -> dict:
    seeds = jax.random.split(jax.random.key(seed), 17)
    return {
        "inputs": bell_draw(seeds[0], (SEQS, LENGTH, D), 1.0, 6.0, ((0, 4), (1, 8)), jnp.float32),
        "cotangent": bell_draw(seeds[1], (SEQS, LENGTH, D), 1.0, 6.0, ((0, 4), (1, 8)), jnp.float32),
        "block_order": jax.vmap(lambda own: jax.random.permutation(own, N_CTX))(jax.random.split(seeds[2], SEQS)).reshape((SEQS, N_CTX)).astype(jnp.int32),
        "doc_cut": touch_ends(jax.random.randint(seeds[3], (SEQS,), LENGTH // 4, 3 * LENGTH // 4 + 1), jax.random.fold_in(seeds[3], 1), LENGTH // 4, (3 * LENGTH // 4 + 1) - 1).astype(jnp.int32),
        "w_qkv": bell_draw(seeds[4], (D, 3 * D), D ** -0.5, 0.125, ((0, 32),)),
        "b_qkv": bell_draw(seeds[5], (3 * D,), 0.5, 3.0, ((0, 32),)),
        "w_dense": bell_draw(seeds[6], (D, D), (D // 32) ** -0.5, 0.75, ((0, 32),)),
        "b_dense": bell_draw(seeds[7], (D,), 1.0, 4.0, ((0, 32),)),
        "w_up": bell_draw(seeds[8], (D, FF), D ** -0.5, 0.125, ((0, 32),)),
        "b_up": bell_draw(seeds[9], (FF,), 0.5, 3.0, ((0, 32),)),
        "w_down": bell_draw(seeds[10], (FF, D), FF ** -0.5, 0.0625, ((0, 32),)),
        "b_down": bell_draw(seeds[11], (D,), 1.0, 4.0, ((0, 32),)),
        "gain_attn": jnp.clip(1.0 + 0.1 * jax.random.normal(seeds[12], (D,), jnp.float32), 0.5, 1.5).astype(jnp.bfloat16),
        "shift_attn": bell_draw(seeds[13], (D,), 0.5, 3.0, ((0, 32),)),
        "gain_mlp": jnp.clip(1.0 + 0.18 * jax.random.normal(seeds[14], (D,), jnp.float32), 0.099609375, 1.8984375).astype(jnp.bfloat16),
        "shift_mlp": bell_draw(seeds[15], (D,), 0.5, 3.0, ((0, 32),)),
    }


norm_eps = 1e-05
large_negative = -1e+30

def normalize_layer(values, gain_vec, shift_vec):
    centre = values - lax.optimization_barrier(jnp.mean(values, -1, keepdims=True))
    inv_std = lax.rsqrt(lax.optimization_barrier(jnp.mean(centre * centre, -1, keepdims=True)) + norm_eps)
    normed = centre * inv_std
    return (normed * gain_vec + shift_vec, normed, inv_std)

def norm_backward_pass(grad_out, normed, inv_std, gain_vec):
    scaled = grad_out * gain_vec
    return (scaled - lax.optimization_barrier(jnp.mean(scaled, -1, keepdims=True)) - normed * lax.optimization_barrier(jnp.mean(scaled * normed, -1, keepdims=True))) * inv_std

def rotate(values, places, direction):
    half_rot = ROT_DIM // 2
    frequency = jnp.power(10000.0, -2.0 * jnp.arange(half_rot).astype(jnp.float32) / ROT_DIM)
    angles = places.astype(jnp.float32)[:, None] * frequency[None, :]
    cos_part = jnp.cos(angles)[:, None, :]
    sine_part = jnp.sin(angles)[:, None, :]
    front_half = values[..., :half_rot]
    back_half = values[..., half_rot:ROT_DIM]
    return jnp.concatenate([front_half * cos_part - direction * back_half * sine_part, back_half * cos_part + direction * front_half * sine_part, values[..., ROT_DIM:]], -1)

def gelu_parts(pre_act):
    normal_cdf = 0.5 * (1.0 + lax.erf(pre_act * 0.7071067811865476))
    density = jnp.exp(-0.5 * pre_act * pre_act) * 0.3989422804014327
    return (pre_act * normal_cdf, normal_cdf + pre_act * density)

def token_places(order_row, cut_value):
    row_index = jnp.arange(LENGTH, dtype=jnp.int32)
    device = row_index // TOK_DEV
    within = row_index % TOK_DEV
    half_dev = TOK_DEV // 2
    first_id = order_row[device]
    block_id = jnp.where(within < half_dev, first_id, 2 * N_CTX - 1 - first_id)
    places = block_id * half_dev + within % half_dev
    return (places, (places >= cut_value).astype(jnp.int32))

def allowed_mask(query_places, query_docs, key_places, key_docs):
    return (key_places[None, :] <= query_places[:, None]) & (key_docs[None, :] == query_docs[:, None])

def round_trip(values):
    return lax.optimization_barrier(values.astype(jnp.bfloat16)).astype(jnp.float32)

def one_sequence(inputs, cotangent, order_row, cut_value, params):
    w_qkv, b_qkv, w_dense, b_dense, w_up, b_up, w_down, b_down, first_gain, first_shift, second_gain, second_shift = params
    places, docs = token_places(order_row, cut_value)
    first_normalized, first_centered_scaled, first_inverse_deviation = normalize_layer(inputs, first_gain, first_shift)
    second_normalized, second_centered_scaled, second_inverse_deviation = normalize_layer(inputs, second_gain, second_shift)
    first_in = first_normalized.astype(jnp.bfloat16)
    second_in = second_normalized.astype(jnp.bfloat16)
    projected = jnp.dot(first_in, w_qkv, preferred_element_type=jnp.float32) + b_qkv
    queries = rotate(projected[:, :D].reshape(LENGTH, HEADS, HEAD_DIM), places, 1.0).astype(jnp.bfloat16)
    keys_all = rotate(projected[:, D:2 * D].reshape(LENGTH, HEADS, HEAD_DIM), places, 1.0).astype(jnp.bfloat16)
    values_all = projected[:, 2 * D:].reshape(LENGTH, HEADS, HEAD_DIM).astype(jnp.bfloat16)
    keys_wide = keys_all.astype(jnp.float32)
    values_wide = values_all.astype(jnp.float32)
    block_rows = math.gcd(LENGTH, 512)
    block_count = LENGTH // block_rows
    score_scale = HEAD_DIM ** (-0.5)

    def block_scores(row_start):
        query_block = lax.dynamic_slice_in_dim(queries, row_start, block_rows, 0).astype(jnp.float32)
        query_places = lax.dynamic_slice_in_dim(places, row_start, block_rows, 0)
        query_docs = lax.dynamic_slice_in_dim(docs, row_start, block_rows, 0)
        allowed = allowed_mask(query_places, query_docs, places, docs)[None]
        scores = jnp.einsum('rhd,khd->hrk', query_block, keys_wide) * score_scale
        return (query_block, allowed, jnp.where(allowed, scores, large_negative))

    def forward_block(block_index):
        row_start = block_index * block_rows
        query_block, allowed, scores = block_scores(row_start)
        highest = lax.optimization_barrier(jnp.max(scores, -1, keepdims=True))
        log_total = highest[..., 0] + jnp.log(lax.optimization_barrier(jnp.sum(jnp.exp(scores - highest), -1)))
        key_probs = jnp.where(allowed, jnp.exp(scores - log_total[..., None]), 0.0)
        attended = jnp.einsum('hrk,khd->rhd', round_trip(key_probs), values_wide).astype(jnp.bfloat16)
        return (attended, log_total)
    attended_blocks, log_blocks = lax.map(forward_block, jnp.arange(block_count, dtype=jnp.int32))
    attended = attended_blocks.reshape(LENGTH, HEADS, HEAD_DIM)
    log_totals = jnp.transpose(log_blocks, (1, 0, 2)).reshape(HEADS, LENGTH)
    attn_flat = attended.reshape(LENGTH, D)
    attn_out = jnp.dot(attn_flat, w_dense, preferred_element_type=jnp.float32) + b_dense
    pre_act = jnp.dot(second_in, w_up, preferred_element_type=jnp.float32) + b_up
    activated, gelu_slope = gelu_parts(pre_act)
    hidden = activated.astype(jnp.bfloat16)
    output = inputs + attn_out + (jnp.dot(hidden, w_down, preferred_element_type=jnp.float32) + b_down)
    grad_rows = cotangent.astype(jnp.bfloat16)
    down_weight_gradient = jnp.dot(hidden.T, grad_rows, preferred_element_type=jnp.float32)
    down_bias_gradient = lax.optimization_barrier(jnp.sum(cotangent, 0))
    d_pre = jnp.dot(grad_rows, w_down.T, preferred_element_type=jnp.float32) * gelu_slope
    up_bias_gradient = lax.optimization_barrier(jnp.sum(d_pre, 0))
    d_pre_b = d_pre.astype(jnp.bfloat16)
    up_weight_gradient = jnp.dot(second_in.T, d_pre_b, preferred_element_type=jnp.float32)
    second_norm_gradient = jnp.dot(d_pre_b, w_up.T, preferred_element_type=jnp.float32)
    dense_weight_gradient = jnp.dot(attn_flat.T, grad_rows, preferred_element_type=jnp.float32)
    dense_bias_gradient = lax.optimization_barrier(jnp.sum(cotangent, 0))
    d_attended = jnp.dot(grad_rows, w_dense.T, preferred_element_type=jnp.float32).astype(jnp.bfloat16)
    d_att_wide = d_attended.reshape(LENGTH, HEADS, HEAD_DIM).astype(jnp.float32)
    correction = jnp.einsum('rhd,rhd->hr', d_att_wide, attended.astype(jnp.float32))

    def backward_block(running, block_index):
        key_grad, value_grad = running
        row_start = block_index * block_rows
        query_block, allowed, scores = block_scores(row_start)
        log_block = lax.dynamic_slice_in_dim(log_totals, row_start, block_rows, 1)
        corr_block = lax.dynamic_slice_in_dim(correction, row_start, block_rows, 1)
        d_block = lax.dynamic_slice_in_dim(d_att_wide, row_start, block_rows, 0)
        key_probs = jnp.where(allowed, jnp.exp(scores - log_block[..., None]), 0.0)
        value_grad = value_grad + jnp.einsum('hrk,rhd->khd', round_trip(key_probs), d_block)
        d_probs = jnp.einsum('rhd,khd->hrk', d_block, values_wide)
        d_scores = round_trip(key_probs * (d_probs - corr_block[..., None]) * score_scale)
        query_grad = jnp.einsum('hrk,khd->rhd', d_scores, keys_wide)
        key_grad = key_grad + jnp.einsum('hrk,rhd->khd', d_scores, query_block)
        return ((key_grad, value_grad), query_grad)
    zero_heads = jnp.zeros((LENGTH, HEADS, HEAD_DIM), jnp.float32)
    (key_grad, value_grad), query_blocks = lax.scan(backward_block, (zero_heads, zero_heads), jnp.arange(block_count, dtype=jnp.int32))
    d_queries = rotate(query_blocks.reshape(LENGTH, HEADS, HEAD_DIM), places, -1.0)
    d_keys = rotate(key_grad, places, -1.0)
    d_proj = jnp.concatenate([d_queries.reshape(LENGTH, D), d_keys.reshape(LENGTH, D), value_grad.reshape(LENGTH, D)], 1)
    projection_bias_gradient = lax.optimization_barrier(jnp.sum(d_proj, 0))
    d_proj_b = d_proj.astype(jnp.bfloat16)
    projection_weight_gradient = jnp.dot(first_in.T, d_proj_b, preferred_element_type=jnp.float32)
    first_norm_gradient = jnp.dot(d_proj_b, w_qkv.T, preferred_element_type=jnp.float32)
    input_gradient = cotangent + norm_backward_pass(first_norm_gradient, first_centered_scaled, first_inverse_deviation, first_gain) + norm_backward_pass(second_norm_gradient, second_centered_scaled, second_inverse_deviation, second_gain)
    gradient_terms = (projection_weight_gradient, projection_bias_gradient, dense_weight_gradient, dense_bias_gradient, up_weight_gradient, up_bias_gradient, down_weight_gradient, down_bias_gradient, lax.optimization_barrier(jnp.sum(first_norm_gradient * first_centered_scaled, 0)), lax.optimization_barrier(jnp.sum(first_norm_gradient, 0)), lax.optimization_barrier(jnp.sum(second_norm_gradient * second_centered_scaled, 0)), lax.optimization_barrier(jnp.sum(second_norm_gradient, 0)))
    return (output, input_gradient, gradient_terms)

def reference(inputs, cotangent, block_order, doc_cut, w_qkv, b_qkv, w_dense, b_dense, w_up, b_up, w_down, b_down, gain_attn, shift_attn, gain_mlp, shift_mlp):
    params = (w_qkv, b_qkv, w_dense, b_dense, w_up, b_up, w_down, b_down, gain_attn, shift_attn, gain_mlp, shift_mlp)
    zero_grads = tuple((jnp.zeros(weight_arg.shape, jnp.float32) for weight_arg in params))

    def accumulate(totals, sequence):
        output, input_gradient, gradient_terms = one_sequence(sequence[0], sequence[1], sequence[2], sequence[3], params)
        return (tuple((summed + extra for summed, extra in zip(totals, gradient_terms))), (output, input_gradient))
    totals, (outputs, d_all) = lax.scan(accumulate, zero_grads, (inputs, cotangent, block_order, doc_cut))
    return (outputs, d_all, totals[0], totals[1], totals[2], totals[3], totals[4], totals[5], totals[6], totals[7], totals[8], totals[9], totals[10], totals[11])
```

```python
import jax
import jax.numpy as jnp
from jax import lax
from jax.experimental import pallas as pl
from jax.experimental.pallas import tpu as pltpu
from jax.sharding import PartitionSpec as P

HEADS = 8
HEAD_DIM = 256
ROT_DIM = 64
HALF = ROT_DIM // 2
NORM_EPS = 1e-05
LARGE_NEGATIVE = -1e30
SCALE = HEAD_DIM ** (-0.5)
f32 = jnp.float32
bf16 = jnp.bfloat16


def dot(a, b):
    return jnp.dot(a, b, preferred_element_type=f32)


def dot_t(a, b):
    return lax.dot_general(a, b, (((1,), (1,)), ((), ())), preferred_element_type=f32)


def t_dot(a, b):
    return lax.dot_general(a, b, (((0,), (0,)), ((), ())), preferred_element_type=f32)


def angles_of(places):
    frequency = jnp.power(10000.0, -2.0 * jnp.arange(HALF).astype(f32) / ROT_DIM)
    return places.astype(f32)[..., None] * frequency


def rotate(values, cos_part, sine_part):
    front = values[..., :HALF]
    back = values[..., HALF:ROT_DIM]
    return jnp.concatenate(
        [front * cos_part - back * sine_part, back * cos_part + front * sine_part, values[..., ROT_DIM:]], -1
    )


def gelu_parts(pre_act):
    normal_cdf = 0.5 * (1.0 + lax.erf(pre_act * 0.7071067811865476))
    density = jnp.exp(-0.5 * pre_act * pre_act) * 0.3989422804014327
    return (pre_act * normal_cdf, normal_cdf + pre_act * density)


def block_places(order, ctx_count, tok_rows):
    half = tok_rows // 2
    within = jnp.arange(tok_rows, dtype=jnp.int32)
    first = order[..., None]
    block = jnp.where(within < half, first, 2 * ctx_count - 1 - first)
    return block * half + within % half


def attention_kernel(x_ref, row_ref, key_ref, cos_ref, sin_ref, out_ref, dk_ref, dv_ref):
    length = x_ref.shape[0]
    hd = HEAD_DIM
    tile = min(256, length)
    lane = lax.broadcasted_iota(jnp.int32, (tile, 128), 1)

    def unrotate(value, rows):
        low = value[:, :128]
        other = jnp.where(lane < HALF, pltpu.roll(low, 128 - HALF, 1), pltpu.roll(low, HALF, 1))
        low = low * cos_ref[rows, :] + other * sin_ref[rows, :]
        return jnp.concatenate([low, value[:, 128:]], 1)

    keys = x_ref[:, hd : 2 * hd]
    values = x_ref[:, 2 * hd : 3 * hd]
    key_place = key_ref[0:1, :]
    for step in range(length // tile):
        rows = slice(step * tile, (step + 1) * tile)
        query = x_ref[rows, 0:hd]
        grad = x_ref[rows, 3 * hd : 4 * hd]
        place = row_ref[rows, 0:1]
        first = row_ref[rows, 1:2]
        allowed = (key_place <= place) & (key_place >= first)
        scores = jnp.where(allowed, dot_t(query, keys) * SCALE, LARGE_NEGATIVE)
        top = jnp.max(scores, 1, keepdims=True)
        weights = jnp.exp(scores - top)
        probs = weights * (1.0 / jnp.sum(weights, 1, keepdims=True))
        probs_b = probs.astype(bf16)
        attended = dot(probs_b, values).astype(bf16)
        out_ref[rows, 0:hd] = attended
        delta = jnp.sum(grad.astype(f32) * attended.astype(f32), 1, keepdims=True)
        d_probs = dot_t(grad, values)
        d_scores = (probs * (d_probs - delta) * SCALE).astype(bf16)
        out_ref[rows, hd : 2 * hd] = unrotate(dot(d_scores, keys), rows).astype(bf16)
        dk = t_dot(d_scores, query)
        dv = t_dot(probs_b, grad)
        if step == 0:
            dk_ref[...] = dk
            dv_ref[...] = dv
        else:
            dk_ref[...] += dk
            dv_ref[...] += dv
    for step in range(length // tile):
        rows = slice(step * tile, (step + 1) * tile)
        out_ref[rows, 2 * hd : 3 * hd] = unrotate(dk_ref[rows, :], rows).astype(bf16)
        out_ref[rows, 3 * hd : 4 * hd] = dv_ref[rows, :].astype(bf16)


def attention(packed, places, cut):
    length = packed.shape[0]
    angle = angles_of(places)
    cos, sin = jnp.cos(angle), jnp.sin(angle)
    rest = 128 - ROT_DIM
    cos_table = jnp.concatenate([cos, cos, jnp.ones((length, rest), f32)], 1)
    sin_table = jnp.concatenate([sin, -sin, jnp.zeros((length, rest), f32)], 1)
    first = jnp.where(places >= cut, cut, 0)
    row_info = jnp.stack([places, first], 1)
    key_info = places[None, :]
    return pl.pallas_call(
        attention_kernel,
        out_shape=jax.ShapeDtypeStruct((length, 4 * HEAD_DIM), bf16),
        in_specs=[pl.BlockSpec(memory_space=pltpu.VMEM)] * 5,
        out_specs=pl.BlockSpec(memory_space=pltpu.VMEM),
        scratch_shapes=[pltpu.VMEM((length, HEAD_DIM), f32), pltpu.VMEM((length, HEAD_DIM), f32)],
        compiler_params=pltpu.CompilerParams(vmem_limit_bytes=48 * 2**20),
        cost_estimate=pl.CostEstimate(
            flops=12 * length * length * HEAD_DIM,
            bytes_accessed=16 * length * HEAD_DIM,
            transcendentals=length * length,
        ),
    )(packed, row_info, key_info, cos_table, sin_table)


def body(
    inputs,
    cotangent,
    block_order,
    doc_cut,
    w_qkv,
    b_qkv,
    w_dense,
    b_dense,
    w_up,
    b_up,
    w_down,
    b_down,
    gain_attn,
    shift_attn,
    gain_mlp,
    shift_mlp,
):
    both = ("ctx", "wsh")
    C = lax.axis_size("ctx")
    W = lax.axis_size("wsh")
    c = lax.axis_index("ctx")
    z = lax.axis_index("wsh")
    T, D = inputs.shape[1:]
    DL = w_qkv.shape[0]
    FL = w_down.shape[0]
    E = D // W
    HL = HEADS // W
    PAIRS = W * HL
    R = C // PAIRS
    ROWS = W * T
    x = inputs[0]
    cot = cotangent[0]

    cut = doc_cut[0]
    ints = jnp.concatenate([block_order[0], (cut // 16)[None], (cut % 16)[None]]).astype(bf16)
    small = [b_qkv, b_dense, b_up, b_down, gain_attn, shift_attn, gain_mlp, shift_mlp, ints]
    sizes = [a.shape[0] for a in small]
    total = sum(sizes)
    width = -(-total // 128) * 128
    pack = jnp.concatenate(small + [jnp.zeros((width - total,), bf16)])
    pack = lax.all_gather(pack[None], both, axis=0, tiled=True)
    starts = [sum(sizes[:i]) for i in range(len(sizes))]
    pieces = [pack[:, s : s + n] for s, n in zip(starts, sizes)]
    bias_qkv, bias_dense, bias_up, bias_down, ga, sa, gm, sm = [p.reshape(-1) for p in pieces[:-1]]
    info = pieces[-1][:W].astype(f32).astype(jnp.int32)
    orders = info[:, :C]
    cuts = info[:, C] * 16 + info[:, C + 1]
    bias_qkv = lax.dynamic_slice_in_dim(bias_qkv.reshape(3, W, E), z, 1, 1).reshape(3 * E)
    bias_up = lax.dynamic_slice_in_dim(bias_up.reshape(C, W, FL), z, 1, 1).reshape(C * FL)

    part_qkv = w_qkv.reshape(DL, 3, W, E).transpose(2, 0, 1, 3).reshape(W, DL, 3 * E)
    part_up = w_up.reshape(DL, C, W, FL).transpose(2, 0, 1, 3).reshape(W, DL, C * FL)
    turned = lax.all_to_all(jnp.concatenate([part_qkv, part_up], 2), "wsh", 0, 0, tiled=True)
    turned = turned.reshape(W * DL, 3 * E + C * FL)
    moves = [(i, (i % C) * W + i // C) for i in range(C * W)]
    back_moves = [(j, i) for i, j in moves]
    full_dense = lax.all_gather(lax.ppermute(w_dense, both, moves), "ctx", axis=0, tiled=True)
    full_down = lax.all_gather(w_down, "ctx", axis=0, tiled=True)
    full_qkv = lax.all_gather(turned[:, : 3 * E], "ctx", axis=0, tiled=True)
    full_up = lax.all_gather(turned[:, 3 * E :], "ctx", axis=0, tiled=True)

    centre = x - jnp.mean(x, -1, keepdims=True)
    inv_std = lax.rsqrt(jnp.mean(centre * centre, -1, keepdims=True) + NORM_EPS)
    normed = centre * inv_std
    xh = lax.all_gather(normed.astype(bf16), "wsh", axis=0, tiled=True)
    g = lax.all_gather(cot.astype(bf16), "wsh", axis=0, tiled=True)
    xh32 = xh.astype(f32)
    h_attn = (xh32 * ga + sa).astype(bf16)
    h_mlp = (xh32 * gm + sm).astype(bf16)

    own_angle = angles_of(block_places(lax.dynamic_index_in_dim(orders, c, 1, False), C, T))[:, :, None, None, :]
    proj = (dot(h_attn, full_qkv) + bias_qkv).reshape(W, T, 3, HL, HEAD_DIM)
    q_k = rotate(proj[:, :, :2], jnp.cos(own_angle), jnp.sin(own_angle)).astype(bf16)
    d_att = dot_t(g, full_dense).astype(bf16).reshape(W, T, 1, HL, HEAD_DIM)
    send = jnp.concatenate([q_k, proj[:, :, 2:].astype(bf16), d_att], 2)
    send = send.transpose(0, 3, 1, 2, 4).reshape(PAIRS, T, 4 * HEAD_DIM)
    if R > 1:
        send = jnp.repeat(send, R, 0)
    packed = lax.all_to_all(send, "ctx", 0, 0, tiled=True).reshape(C * T, 4 * HEAD_DIM)
    seq = c // R // HL
    seq_order = lax.dynamic_index_in_dim(orders, seq, 0, False)
    seq_cut = lax.dynamic_index_in_dim(cuts, seq, 0, False)
    result = attention(packed, block_places(seq_order, C, T).reshape(-1), seq_cut)
    result = lax.all_to_all(result.reshape(C, T, 4 * HEAD_DIM), "ctx", 0, 0, tiled=True)
    if R > 1:
        result = result.reshape(PAIRS, R, T, 4 * HEAD_DIM)[:, 0]
    result = result.reshape(W, HL, T, 4, HEAD_DIM).transpose(3, 0, 2, 1, 4).reshape(4, ROWS, E)
    attended = result[0]
    d_proj = result[1:].transpose(1, 0, 2).reshape(ROWS, 3 * E)

    pre = dot(h_mlp, full_up) + bias_up
    activated, slope = gelu_parts(pre)
    hidden = activated.astype(bf16)
    d_pre = dot_t(g, full_down) * slope
    d_pre_b = d_pre.astype(bf16)
    gw_down = t_dot(hidden, g).astype(bf16)
    gw_up = t_dot(h_mlp, d_pre_b).astype(bf16)
    d_h_mlp = dot_t(d_pre_b, full_up)

    def scatter(value, axis):
        return lax.psum_scatter(value, axis, scatter_dimension=0, tiled=True)

    out_part = dot(hidden, full_down) + dot(attended, full_dense)
    out_sum = scatter(out_part.astype(bf16), "wsh").astype(f32)
    output = x + out_sum + bias_dense + bias_down

    gw_dense = t_dot(attended, g).astype(bf16)
    gw_qkv = t_dot(h_attn, d_proj).astype(bf16)
    d_h_attn = dot_t(d_proj, full_qkv)

    e = scatter((d_h_attn * ga + d_h_mlp * gm).astype(bf16), "wsh").astype(f32)
    input_gradient = (
        cot + (e - jnp.mean(e, -1, keepdims=True) - normed * jnp.mean(e * normed, -1, keepdims=True)) * inv_std
    )

    grad_down = scatter(gw_down, "ctx").astype(f32)
    grad_dense = lax.ppermute(scatter(gw_dense, "ctx"), both, back_moves).astype(f32)
    own_up = scatter(gw_up, "ctx").reshape(W, DL, C * FL)
    own_qkv = scatter(gw_qkv, "ctx").reshape(W, DL, 3 * E)
    turned = lax.all_to_all(jnp.concatenate([own_qkv, own_up], 2), "wsh", 0, 0, tiled=True).astype(f32)
    grad_qkv = turned[:, :, : 3 * E].reshape(W, DL, 3, E).transpose(1, 2, 0, 3).reshape(DL, 3 * D)
    grad_up = turned[:, :, 3 * E :].reshape(W, DL, C, FL).transpose(1, 2, 0, 3).reshape(DL, C * W * FL)

    gb_qkv = jnp.zeros((3, W, E), f32)
    gb_qkv = lax.dynamic_update_slice_in_dim(gb_qkv, jnp.sum(d_proj.astype(f32), 0).reshape(3, 1, E), z, 1)
    gb_up = jnp.zeros((C, W, FL), f32)
    gb_up = lax.dynamic_update_slice_in_dim(gb_up, jnp.sum(d_pre, 0).reshape(C, 1, FL), z, 1)
    vectors = [
        gb_qkv,
        jnp.sum(cot, 0),
        gb_up,
        jnp.sum(d_h_attn * xh32, 0),
        jnp.sum(d_h_attn, 0),
        jnp.sum(d_h_mlp * xh32, 0),
        jnp.sum(d_h_mlp, 0),
    ]
    vectors = [v.reshape(C * W, -1) for v in vectors]
    lengths = [v.shape[1] for v in vectors]
    summed = jnp.sum(lax.all_to_all(jnp.concatenate(vectors, 1), both, 0, 0, tiled=True), 0)
    marks = [sum(lengths[:i]) for i in range(len(lengths))]
    gb_qkv, gb_dense, gb_up, g_ga, g_sa, g_gm, g_sm = [summed[m : m + n] for m, n in zip(marks, lengths)]
    return (
        output[None],
        input_gradient[None],
        grad_qkv,
        gb_qkv,
        grad_dense,
        gb_dense,
        grad_up,
        gb_up,
        grad_down,
        gb_dense,
        g_ga,
        g_sa,
        g_gm,
        g_sm,
    )


def solution(mesh):
    tokens = P("wsh", "ctx", None)
    matrix = P(("ctx", "wsh"), None)
    vector = P(("ctx", "wsh"))
    pairs = (matrix, vector) * 4
    return jax.shard_map(
        body,
        mesh=mesh,
        in_specs=(tokens, tokens, P("wsh", None), P("wsh")) + pairs + (vector,) * 4,
        out_specs=(tokens, tokens) + pairs + (vector,) * 4,
        check_vma=False,
    )
```

```python
import jax
import jax.numpy as jnp
from jax import lax
from jax.experimental import pallas as pl
from jax.experimental.pallas import tpu as pltpu
from jax.sharding import Mesh
from jax.sharding import PartitionSpec as P

HEADS = 8
HEAD_DIM = 256
ROT_DIM = 64
HALF = ROT_DIM // 2
NORM_EPS = 1e-05
LARGE_NEGATIVE = -1e30
SCALE = HEAD_DIM ** (-0.5)
f32 = jnp.float32
bf16 = jnp.bfloat16


def dot(a, b):
    return jnp.dot(a, b, preferred_element_type=f32)


def dot_t(a, b):
    return lax.dot_general(a, b, (((1,), (1,)), ((), ())), preferred_element_type=f32)


def t_dot(a, b):
    return lax.dot_general(a, b, (((0,), (0,)), ((), ())), preferred_element_type=f32)


def angles_of(places):
    frequency = jnp.power(10000.0, -2.0 * jnp.arange(HALF).astype(f32) / ROT_DIM)
    return places.astype(f32)[..., None] * frequency


def gelu_parts(pre_act):
    normal_cdf = 0.5 * (1.0 + lax.erf(pre_act * 0.7071067811865476))
    density = jnp.exp(-0.5 * pre_act * pre_act) * 0.3989422804014327
    return (pre_act * normal_cdf, normal_cdf + pre_act * density)


def block_places(order, ctx_count, tok_rows):
    half = tok_rows // 2
    within = jnp.arange(tok_rows, dtype=jnp.int32)
    first = order[..., None]
    block = jnp.where(within < half, first, 2 * ctx_count - 1 - first)
    return block * half + within % half


VMEM_LIMIT = 56 * 2**20


def rotary_tables(places, direction):
    angle = angles_of(places)
    cos, sin = jnp.cos(angle), jnp.sin(angle) * direction
    rest = 128 - ROT_DIM
    ones = jnp.ones((places.shape[0], rest), f32)
    return jnp.concatenate([cos, cos, ones], 1), jnp.concatenate([-sin, sin, 0.0 * ones], 1)


def turn(value, cos, sin):
    low = value[:, :128]
    lane = lax.broadcasted_iota(jnp.int32, low.shape, 1)
    other = jnp.where(lane < HALF, pltpu.roll(low, 128 - HALF, 1), pltpu.roll(low, HALF, 1))
    return jnp.concatenate([low * cos + other * sin, value[:, 128:]], 1)


class Columns:
    def __init__(self, array, unit, j):
        self.array, self.unit, self.j = array, unit, j
        self.shape = array.shape[:-1] + (unit,)
        self.dtype = array.dtype
        self.size = array.size // array.shape[-1] * unit


def columns(array, unit, first, last):
    return [Columns(array, unit, j) for j in range(first, last)]


def call(kernel, outs, operands, flops, scratch=(), scalar=None):
    moved = sum(o.size * o.dtype.itemsize for o in list(operands) + list(outs))
    in_specs, arrays = [], []
    if scalar is not None:
        in_specs.append(pl.BlockSpec(memory_space=pltpu.SMEM))
        arrays.append(scalar.reshape(1).astype(jnp.int32))
    for operand in operands:
        if isinstance(operand, Columns):
            lead = (0,) * (len(operand.shape) - 1)
            in_specs.append(pl.BlockSpec(operand.shape, lambda i, lead=lead, j=operand.j: lead + (j,)))
            arrays.append(operand.array)
        else:
            zero = (0,) * len(operand.shape)
            in_specs.append(pl.BlockSpec(operand.shape, lambda i, zero=zero: zero))
            arrays.append(operand)
    out_specs = [pl.BlockSpec(o.shape, lambda i, zero=(0,) * len(o.shape): zero) for o in outs]
    return pl.pallas_call(
        kernel,
        grid=(1,),
        out_shape=outs,
        in_specs=in_specs,
        out_specs=out_specs,
        scratch_shapes=list(scratch),
        compiler_params=pltpu.CompilerParams(vmem_limit_bytes=VMEM_LIMIT),
        cost_estimate=pl.CostEstimate(flops=flops, bytes_accessed=moved, transcendentals=0),
    )(*arrays)


def kept_block(p, count, core):
    half = count // 2
    return 2 * (p % half) + (core if p < half else 1 - core)


def kept_difference(p, count):
    half = count // 2
    return 2 * (p % half) + p // half


def at(index, size):
    return pl.ds(pl.multiple_of(index * size, size), size)


def shaped(shape, dtype):
    return jax.ShapeDtypeStruct(shape, dtype)


def attention_kernel(x_ref, row_ref, key_ref, cos_ref, sin_ref, out_ref, dk_ref, dv_ref):
    length = x_ref.shape[0]
    hd = HEAD_DIM
    tile = min(256, length)
    keys = x_ref[:, hd : 2 * hd]
    values = x_ref[:, 2 * hd : 3 * hd]
    key_place = key_ref[0:1, :]
    for step in range(length // tile):
        rows = slice(step * tile, (step + 1) * tile)
        query = x_ref[rows, 0:hd]
        grad = x_ref[rows, 3 * hd : 4 * hd]
        place = row_ref[rows, 0:1]
        first = row_ref[rows, 1:2]
        allowed = (key_place <= place) & (key_place >= first)
        scores = jnp.where(allowed, dot_t(query, keys) * SCALE, LARGE_NEGATIVE)
        top = jnp.max(scores, 1, keepdims=True)
        weights = jnp.exp(scores - top)
        probs = weights * (1.0 / jnp.sum(weights, 1, keepdims=True))
        probs_b = probs.astype(bf16)
        attended = dot(probs_b, values).astype(bf16)
        out_ref[rows, 0:hd] = attended
        delta = jnp.sum(grad.astype(f32) * attended.astype(f32), 1, keepdims=True)
        d_probs = dot_t(grad, values)
        d_scores = (probs * (d_probs - delta) * SCALE).astype(bf16)
        d_query = dot(d_scores, keys)
        out_ref[rows, hd : 2 * hd] = turn(d_query, cos_ref[rows, :], sin_ref[rows, :]).astype(bf16)
        dk = t_dot(d_scores, query)
        dv = t_dot(probs_b, grad)
        if step == 0:
            dk_ref[...] = dk
            dv_ref[...] = dv
        else:
            dk_ref[...] += dk
            dv_ref[...] += dv
    for step in range(length // tile):
        rows = slice(step * tile, (step + 1) * tile)
        out_ref[rows, 2 * hd : 3 * hd] = turn(dk_ref[rows, :], cos_ref[rows, :], sin_ref[rows, :]).astype(bf16)
        out_ref[rows, 3 * hd : 4 * hd] = dv_ref[rows, :].astype(bf16)


def attention(packed, places, cut):
    length = packed.shape[0]
    cos_table, sin_table = rotary_tables(places, -1.0)
    first = jnp.where(places >= cut, cut, 0)
    row_info = jnp.stack([places, first], 1)
    operands = (packed, row_info, places[None, :], cos_table, sin_table)
    scratch = [pltpu.VMEM((length, HEAD_DIM), f32), pltpu.VMEM((length, HEAD_DIM), f32)]
    outs = [shaped((length, 4 * HEAD_DIM), bf16)]
    return call(attention_kernel, outs, operands, 12 * length * length * HEAD_DIM, scratch)[0]


def project(acts, gain, shift_by, held, bias, cos, sin, part, tokens, index):
    rows, width = acts.shape[0], acts.shape[1] // 2
    count, unit = held.shape[0], held.shape[2] // 8
    seqs = rows // tokens
    hd = HEAD_DIM
    heads = unit // hd
    pieces = width // unit
    size = part // pieces

    def kernel(*refs):
        index_ref, acts_ref, gain_ref, shift_ref, bias_ref, cos_ref, sin_ref = refs[:7]
        w_refs, dense_in_ref = refs[7:10], refs[10]
        send_ref, h_ref, dense_ref = refs[11:]
        core = index_ref[0] & 1
        for p in range(count):
            for j in range(pieces):
                block = dense_in_ref[p, j * size : (j + 1) * size, :]
                dense_ref[p * size : (p + 1) * size, j * unit : (j + 1) * unit] = block
            cols = at(kept_block(p, count, core), part)
            h = acts_ref[:, cols].astype(f32) * gain_ref[0:1, cols] + shift_ref[0:1, cols]
            h_ref[:, p * part : (p + 1) * part] = h.astype(bf16)
        for head in range(heads):
            for piece in range(3):
                start = (head * 3 + piece) * hd
                total = jnp.broadcast_to(bias_ref[0:1, start : start + hd], (rows, hd))
                w_ref, start = w_refs[start // unit], start % unit
                for p in range(count):
                    block = w_ref[kept_block(p, count, core), :part, start : start + hd]
                    total = total + dot(h_ref[:, p * part : (p + 1) * part], block)
                if piece < 2:
                    total = turn(total, cos_ref[...], sin_ref[...])
                send_ref[:, head, :, piece * hd : (piece + 1) * hd] = total.astype(bf16).reshape(seqs, tokens, hd)
            d_att = dot_t(acts_ref[:, width:], dense_ref[head * hd : (head + 1) * hd, :])
            send_ref[:, head, :, 3 * hd :] = d_att.astype(bf16).reshape(seqs, tokens, hd)

    outs = [
        shaped((seqs, heads, tokens, 4 * hd), bf16),
        shaped((rows, width), bf16),
        shaped((unit, width), bf16),
    ]
    operands = [acts, gain[None], shift_by[None], bias[None], cos, sin]
    operands += columns(held, unit, 0, 4)
    return call(kernel, outs, operands, 8 * rows * width * unit, scalar=index)


def feed_forward(acts, gain, shift_by, held, bias, down_blocks, part, index):
    rows, width = acts.shape[0], acts.shape[1] // 2
    count, unit = held.shape[0], held.shape[2] // 8
    size = down_blocks[0].shape[0]
    hidden_n = 4 * unit
    tile = 256

    def kernel(*refs):
        index_ref, acts_ref, gain_ref, shift_ref, bias_ref = refs[:5]
        up_refs = refs[5:9]
        down_refs = refs[9 : 9 + count]
        h_ref, hidden_ref, d_pre_ref, out_ref, sum_ref, down_ref = refs[9 + count :]
        core = index_ref[0] & 1
        for p in range(count):
            down_ref[at(index_ref[0] ^ kept_difference(p, count), size), :] = down_refs[p][...]
            cols = at(kept_block(p, count, core), part)
            h = acts_ref[:, cols].astype(f32) * gain_ref[0:1, cols] + shift_ref[0:1, cols]
            h_ref[:, p * part : (p + 1) * part] = h.astype(bf16)
        for step in range(hidden_n // tile):
            cols = slice(step * tile, (step + 1) * tile)
            up_ref, start = up_refs[step * tile // unit], step * tile % unit
            pre = jnp.broadcast_to(bias_ref[0:1, cols], (rows, tile))
            for p in range(count):
                block = up_ref[kept_block(p, count, core), :part, start : start + tile]
                pre = pre + dot(h_ref[:, p * part : (p + 1) * part], block)
            activated, slope = gelu_parts(pre)
            hidden_ref[:, cols] = activated.astype(bf16)
            d_pre = dot_t(acts_ref[:, width:], down_ref[cols, :]) * slope
            sum_ref[0:1, cols] = jnp.sum(d_pre, 0, keepdims=True)
            d_pre_ref[:, cols] = d_pre.astype(bf16)
        for step in range(width // 256):
            cols = slice(step * 256, (step + 1) * 256)
            out_ref[:, cols] = dot(hidden_ref[...], down_ref[:, cols])

    outs = [
        shaped((rows, width), bf16),
        shaped((rows, hidden_n), bf16),
        shaped((rows, hidden_n), bf16),
        shaped((rows, width), f32),
        shaped((1, hidden_n), f32),
    ]
    operands = [acts, gain[None], shift_by[None], bias[None]] + columns(held, unit, 4, 8) + list(down_blocks)
    scratch = [pltpu.VMEM((hidden_n, width), bf16)]
    return call(kernel, outs, operands, 6 * rows * width * hidden_n, scratch, scalar=index)


def input_terms(d_out, held, first, acts, gain, part, e_before=None):
    rows, width = acts.shape[0], acts.shape[1] // 2
    count, unit = held.shape[0], held.shape[2] // 8
    units = d_out.shape[1] // unit

    def kernel(*refs):
        d_out_ref, acts_ref, gain_ref = refs[:3]
        w_refs = refs[3 : 3 + units]
        e_ref, sum_ref = refs[-2:]
        for p in range(count):
            cols = slice(p * part, (p + 1) * part)
            d_h = dot_t(d_out_ref[:, :unit], w_refs[0][p, :part, :])
            for j in range(1, units):
                d_h = d_h + dot_t(d_out_ref[:, j * unit : (j + 1) * unit], w_refs[j][p, :part, :])
            sum_ref[0:1, cols] = jnp.sum(d_h * acts_ref[:, cols].astype(f32), 0, keepdims=True)
            sum_ref[1:2, cols] = jnp.sum(d_h, 0, keepdims=True)
            e = d_h * gain_ref[0:1, cols]
            if e_before is not None:
                e = e + refs[3 + units][:, cols]
            e_ref[:, cols] = e.astype(e_ref.dtype)

    outs = [shaped((rows, width), f32 if e_before is None else bf16), shaped((2, width), f32)]
    operands = [d_out, acts, gain[None]] + columns(held, unit, first, first + units)
    if e_before is not None:
        operands.append(e_before)
    return call(kernel, outs, operands, 2 * rows * width * d_out.shape[1])


def split_columns(w_qkv, w_up, wsh, ctx):
    rows = w_qkv.shape[0]
    width = w_qkv.shape[1] // 3
    hd = HEAD_DIM
    heads = HEADS // wsh
    fl = w_up.shape[1] // (ctx * wsh)

    def kernel(qkv_ref, up_ref, out_ref):
        for z in range(wsh):
            for head in range(heads):
                for piece in range(3):
                    start = piece * width + (z * heads + head) * hd
                    to = (head * 3 + piece) * hd
                    out_ref[z, :, to : to + hd] = qkv_ref[:, start : start + hd]
            out_ref[z, :, 3 * heads * hd :] = jnp.concatenate(
                [up_ref[:, (c * wsh + z) * fl : (c * wsh + z + 1) * fl] for c in range(ctx)], 1
            )

    outs = [shaped((wsh, rows, 3 * heads * hd + ctx * fl), bf16)]
    return call(kernel, outs, (w_qkv, w_up), 0)[0]


def join_qkv(parts, columns):
    wsh, rows, _ = parts.shape
    hd = HEAD_DIM
    heads = HEADS // wsh

    def kernel(in_ref, out_ref):
        for z in range(wsh):
            for head in range(heads):
                for piece in range(3):
                    to = piece * HEADS * hd + (z * heads + head) * hd
                    start = (head * 3 + piece) * hd
                    out_ref[:, to : to + hd] = in_ref[z, :, start : start + hd].astype(f32)

    return call(kernel, [shaped((rows, wsh * columns), f32)], (parts,), 0)[0]


def join_up(parts, first, ctx):
    wsh, rows, columns = parts.shape
    fl = (columns - first) // ctx

    def kernel(in_ref, out_ref):
        for c in range(ctx):
            start = first + c * fl
            out_ref[:, c * wsh * fl : (c + 1) * wsh * fl] = jnp.concatenate(
                [in_ref[z, :, start : start + fl].astype(f32) for z in range(wsh)], 1
            )

    return call(kernel, [shaped((rows, wsh * (columns - first)), f32)], (parts,), 0)[0]


def unpack(result):
    seqs, heads, tokens, _ = result.shape
    hd = HEAD_DIM
    rows = seqs * tokens

    def kernel(in_ref, att_ref, proj_ref, sum_ref):
        for head in range(heads):
            value = in_ref[:, head].reshape(rows, 4 * hd)
            att_ref[:, head * hd : (head + 1) * hd] = value[:, :hd]
            proj_ref[:, head * 3 * hd : (head + 1) * 3 * hd] = value[:, hd:]
            sum_ref[0:1, head * 3 * hd : (head + 1) * 3 * hd] = jnp.sum(value[:, hd:].astype(f32), 0, keepdims=True)

    outs = [
        shaped((rows, heads * hd), bf16),
        shaped((rows, heads * 3 * hd), bf16),
        shaped((1, heads * 3 * hd), f32),
    ]
    return call(kernel, outs, (result,), 0)


CTX = ("chip", "core")


def after(value, *others):
    return lax.optimization_barrier((value,) + others)[0]


def hop(value):
    return lax.ppermute(value, "core", [(0, 1), (1, 0)])


def exchange(value, axis):
    return lax.all_to_all(value, axis, 0, 0, tiled=True)


def chip_hop(value, k):
    n = lax.axis_size("chip")
    return lax.ppermute(value, "chip", [(i, i ^ k) for i in range(n)])


def shift(value, step):
    n = lax.axis_size("wsh")
    return lax.ppermute(value, "wsh", [(i, (i + step) % n) for i in range(n)])


def chip_blocks(block):
    return [block] + [chip_hop(block, k) for k in range(1, lax.axis_size("chip"))]


def with_other_core(own):
    return list(own) + [hop(value) for value in own]


def sum_arrived(value):
    return jnp.sum(value.astype(f32), 0).astype(bf16)


def over_cores(value):
    core = lax.axis_index("core")
    away = hop(lax.dynamic_index_in_dim(value, 1 - core, 1, False))
    return (lax.dynamic_index_in_dim(value, core, 1, False).astype(f32) + away.astype(f32)).astype(bf16)


def hop_terms(terms):
    return [chip_hop(term, k) for k, term in enumerate(terms) if k]


def sum_terms(own, arrived):
    total = own.astype(f32)
    for term in arrived:
        total = total + term.astype(f32)
    return total.astype(bf16)


def body(
    inputs,
    cotangent,
    block_order,
    doc_cut,
    w_qkv,
    b_qkv,
    w_dense,
    b_dense,
    w_up,
    b_up,
    w_down,
    b_down,
    gain_attn,
    shift_attn,
    gain_mlp,
    shift_mlp,
):
    both = CTX + ("wsh",)
    C = lax.axis_size(CTX)
    W = lax.axis_size("wsh")
    core = lax.axis_index("core")
    c = lax.axis_index(CTX)
    z = lax.axis_index("wsh")
    T, D = inputs.shape[1:]
    DL = w_qkv.shape[0]
    FL = w_down.shape[0]
    E = D // W
    HL = HEADS // W
    PAIRS = W * HL
    R = C // PAIRS
    PART = D // C
    x = inputs[0]
    cot = cotangent[0]

    moves = [(i, (i % C) * W + i // C) for i in range(C * W)]
    back_moves = [(j, i) for i, j in moves]
    own_down = chip_blocks(w_down)
    moved_dense = lax.ppermute(w_dense, both, moves)

    centre = x - jnp.mean(x, -1, keepdims=True)
    inv_std = lax.rsqrt(jnp.mean(centre * centre, -1, keepdims=True) + NORM_EPS)
    normed = centre * inv_std
    acts = jnp.concatenate([normed.astype(bf16), cot.astype(bf16)], 1)
    cut = doc_cut[0]
    ints = jnp.concatenate([block_order[0], (cut // 16)[None], (cut % 16)[None]]).astype(bf16)
    small = [b_qkv, b_dense, b_up, b_down, gain_attn, shift_attn, gain_mlp, shift_mlp, ints]
    sizes = [a.shape[0] for a in small]
    starts = [sum(sizes[:i]) for i in range(len(sizes))]
    rider = jnp.concatenate(small + [jnp.zeros((3 * E - sum(sizes),), bf16)])
    turned = exchange(split_columns(w_qkv, w_up, W, C), "wsh")
    rider = jnp.broadcast_to(rider, (16, 3 * E))
    riders = jnp.broadcast_to(rider[:1], (16, 3 * E))
    for k in range(1, W):
        riders = lax.dynamic_update_slice_in_dim(riders, shift(rider, k)[:1], (z - k) % W, 0)
    riders = lax.dynamic_update_slice_in_dim(riders, rider[:1], z, 0)
    turned, acts, riders, moved_dense, *own_down = lax.optimization_barrier((turned, acts, riders, moved_dense, *own_down))
    dense_part = moved_dense.reshape(DL, W, E).transpose(1, 0, 2).reshape(W * DL, E)
    turned = turned.reshape(W * DL, 7 * E)
    held = jnp.concatenate([turned[:, : 3 * E], dense_part, turned[:, 3 * E :]], 1)
    held = jnp.concatenate([held, jnp.pad(riders, ((0, 0), (0, 5 * E)))], 0)
    held = lax.all_gather(held[None], CTX, axis=0, tiled=True)
    acts_all = jnp.zeros((W, T, 2 * D), bf16)
    acts_all = lax.dynamic_update_slice_in_dim(acts_all, acts[None], z, 0)
    for k in range(1, W):
        acts_all = lax.dynamic_update_slice_in_dim(acts_all, shift(acts, k)[None], (z - k) % W, 0)
    acts = acts_all.reshape(W * T, 2 * D)
    g = acts[:, D:]
    blocks_down = with_other_core(own_down)
    held, acts, *blocks_down = lax.optimization_barrier((held, acts, *blocks_down))
    pack = held[:, W * DL : W * DL + W, : 3 * E]
    pieces = [pack[:, :, s : s + n].astype(f32) for s, n in zip(starts, sizes)]
    bias_qkv, bias_dense, bias_up, bias_down, ga, sa, gm, sm = [p.reshape(-1) for p in pieces[:8]]
    info = pieces[-1][0].astype(jnp.int32)
    orders = info[:, :C]
    cuts = info[:, C] * 16 + info[:, C + 1]
    bias_qkv = lax.dynamic_index_in_dim(bias_qkv.reshape(3, W, HL, HEAD_DIM), z, 1, False).transpose(1, 0, 2).reshape(3 * E)
    bias_up = lax.dynamic_index_in_dim(pieces[2], z, 1, False).reshape(C * FL)

    own_places = block_places(lax.dynamic_index_in_dim(orders, c, 1, False), C, T).reshape(-1)
    own_cos, own_sin = rotary_tables(own_places, 1.0)
    send, h_attn, full_dense = project(acts, ga, sa, held, bias_qkv, own_cos, own_sin, PART, T, c)
    send = send.reshape(PAIRS, T, 4 * HEAD_DIM)
    if R > 1:
        send = jnp.repeat(send, R, 0)
    packed = exchange(send, CTX).reshape(C * T, 4 * HEAD_DIM)

    h_mlp, hidden, d_pre, out_mlp, sum_pre = feed_forward(
        after(acts, send), gm, sm, held, bias_up, blocks_down, PART, c
    )
    seq = c // R // HL
    seq_order = lax.dynamic_index_in_dim(orders, seq, 0, False)
    seq_cut = lax.dynamic_index_in_dim(cuts, seq, 0, False)
    result = attention(after(packed, d_pre), block_places(seq_order, C, T).reshape(-1), seq_cut)

    h_late = after(h_mlp, result)
    result = exchange(result.reshape(C, T, 4 * HEAD_DIM), CTX)
    away_up = hop(t_dot(h_late[:, D // 2 :], d_pre).astype(bf16))
    gw_down = t_dot(after(hidden, away_up), g).astype(bf16)
    kept_up = (t_dot(h_late[:, : D // 2], d_pre) + away_up.astype(f32)).astype(bf16)
    kept_down = over_cores(gw_down.reshape(C // 2, 2, FL, D))
    result = after(result, kept_up, kept_down)
    arrived_up = exchange(after(kept_up, result).reshape(C // 2, PART, C * FL), "chip")
    if R > 1:
        result = result.reshape(PAIRS, R, T, 4 * HEAD_DIM)[:, 0]
    attended, d_proj, sum_proj = unpack(result.reshape(W, HL, T, 4 * HEAD_DIM))
    away_qkv = t_dot(h_attn[:, D // 2 :], d_proj).astype(bf16)
    out_part = (out_mlp + dot(after(attended, away_qkv), full_dense)).astype(bf16)
    away_here = hop(away_qkv)
    out_sum = lax.psum_scatter(out_part.reshape(W * T, D), "wsh", scatter_dimension=0, tiled=True)
    gw_dense = t_dot(attended, g).astype(bf16)
    kept_qkv = (t_dot(after(h_attn, out_part)[:, : D // 2], d_proj) + away_here.astype(f32)).astype(bf16)
    e_mlp, sums_mlp = input_terms(after(d_pre, kept_qkv), held, 4, acts, gm, PART)
    e_mlp, arrived_up = lax.optimization_barrier((e_mlp, arrived_up))
    arrived_qkv = exchange(after(kept_qkv, arrived_up).reshape(C // 2, PART, 3 * E), "chip")
    e_part, sums_attn = input_terms(d_proj, held, 0, acts, ga, PART, e_mlp)
    e_part, out_sum = lax.optimization_barrier((e_part, out_sum))
    e_sum = lax.psum_scatter(e_part, "wsh", scatter_dimension=0, tiled=True)

    kept_dense = over_cores(after(gw_dense, e_part).reshape(C // 2, 2, DL, D))
    own_up = sum_arrived(after(arrived_up, e_part))
    arrived_qkv = after(arrived_qkv, own_up, kept_dense)
    own_grads = jnp.concatenate([sum_arrived(arrived_qkv), own_up], 1)
    back = exchange(own_grads.reshape(W, DL, 7 * E), "wsh")
    kept_down = after(kept_down, arrived_qkv)
    terms = [lax.dynamic_index_in_dim(kept_down, lax.axis_index("chip") ^ k, 0, False) for k in range(C // 2)]
    grad_down = terms[0].astype(f32)
    for term in hop_terms(terms):
        grad_down = grad_down + term.astype(f32)
    terms = [lax.dynamic_index_in_dim(kept_dense, lax.axis_index("chip") ^ k, 0, False) for k in range(C // 2)]
    grad_dense = lax.ppermute(sum_terms(terms[0], hop_terms(terms)), both, back_moves).astype(f32)

    output = x + out_sum.astype(f32) + (bias_dense + bias_down)
    e = e_sum.astype(f32)
    input_gradient = (
        cot + (e - jnp.mean(e, -1, keepdims=True) - normed * jnp.mean(e * normed, -1, keepdims=True)) * inv_std
    )
    grad_qkv = join_qkv(after(back, grad_down), 3 * E)
    grad_up = join_up(back, 3 * E, C)

    sum_proj = sum_proj.reshape(HL, 3, HEAD_DIM).transpose(1, 0, 2).reshape(3, 1, E)
    gb_qkv = lax.dynamic_update_slice_in_dim(jnp.zeros((3, W, E), f32), sum_proj, z, 1).reshape(C * W, -1)
    gb_up = lax.dynamic_update_slice_in_dim(jnp.zeros((C, W, FL), f32), sum_pre.reshape(C, 1, FL), z, 1)
    gb_up = gb_up.reshape(C * W, FL)
    by_width = jnp.concatenate([sums_attn, sums_mlp, jnp.sum(cot, 0, keepdims=True)], 0)
    by_width = by_width.reshape(5, C * W, DL).transpose(1, 0, 2).reshape(C * W, 5 * DL)
    vectors = jnp.concatenate([gb_up, gb_qkv, by_width], 1)
    summed = jnp.sum(exchange(after(vectors, own_grads), both), 0)
    n_up, n_qkv = gb_up.shape[1], gb_qkv.shape[1]
    gb_up, gb_qkv = summed[:n_up], summed[n_up : n_up + n_qkv]
    g_ga, g_sa, g_gm, g_sm, gb_dense = [
        summed[n_up + n_qkv + i * DL : n_up + n_qkv + (i + 1) * DL] for i in range(5)
    ]
    return (
        output[None],
        input_gradient[None],
        grad_qkv,
        gb_qkv,
        grad_dense,
        gb_dense,
        grad_up,
        gb_up,
        grad_down,
        gb_dense,
        g_ga,
        g_sa,
        g_gm,
        g_sm,
    )


def solution(mesh):
    ctx, wsh = mesh.shape["ctx"], mesh.shape["wsh"]
    split = Mesh(mesh.devices.reshape(ctx // 2, 2, wsh), CTX + ("wsh",))
    tokens = P("wsh", CTX, None)
    matrix = P(CTX + ("wsh",), None)
    vector = P(CTX + ("wsh",))
    pairs = (matrix, vector) * 4
    return jax.shard_map(
        body,
        mesh=split,
        in_specs=(tokens, tokens, P("wsh", None), P("wsh")) + pairs + (vector,) * 4,
        out_specs=(tokens, tokens) + pairs + (vector,) * 4,
        check_vma=False,
    )
```

```python
import jax
import jax.numpy as jnp
from jax import lax
from jax.experimental import pallas as pl
from jax.experimental.pallas import tpu as pltpu
from jax.sharding import Mesh
from jax.sharding import PartitionSpec as P

HEADS = 8
HEAD_DIM = 256
ROT_DIM = 64
HALF = ROT_DIM // 2
NORM_EPS = 1e-05
LARGE_NEGATIVE = -1e30
SCALE = HEAD_DIM ** (-0.5)
f32 = jnp.float32
bf16 = jnp.bfloat16


def dot(a, b):
    return jnp.dot(a, b, preferred_element_type=f32)


def dot_t(a, b):
    return lax.dot_general(a, b, (((1,), (1,)), ((), ())), preferred_element_type=f32)


def t_dot(a, b):
    return lax.dot_general(a, b, (((0,), (0,)), ((), ())), preferred_element_type=f32)


def angles_of(places):
    frequency = jnp.power(10000.0, -2.0 * jnp.arange(HALF).astype(f32) / ROT_DIM)
    return places.astype(f32)[..., None] * frequency


def gelu_parts(pre_act):
    normal_cdf = 0.5 * (1.0 + lax.erf(pre_act * 0.7071067811865476))
    density = jnp.exp(-0.5 * pre_act * pre_act) * 0.3989422804014327
    return (pre_act * normal_cdf, normal_cdf + pre_act * density)


def block_places(order, ctx_count, tok_rows):
    half = tok_rows // 2
    within = jnp.arange(tok_rows, dtype=jnp.int32)
    first = order[..., None]
    block = jnp.where(within < half, first, 2 * ctx_count - 1 - first)
    return block * half + within % half


VMEM_LIMIT = 56 * 2**20


def rotary_tables(places, direction):
    angle = angles_of(places)
    cos, sin = jnp.cos(angle), jnp.sin(angle) * direction
    rest = 128 - ROT_DIM
    ones = jnp.ones((places.shape[0], rest), f32)
    return jnp.concatenate([cos, cos, ones], 1), jnp.concatenate([-sin, sin, 0.0 * ones], 1)


def turn(value, cos, sin):
    low = value[:, :128]
    lane = lax.broadcasted_iota(jnp.int32, low.shape, 1)
    other = jnp.where(lane < HALF, pltpu.roll(low, 128 - HALF, 1), pltpu.roll(low, HALF, 1))
    return jnp.concatenate([low * cos + other * sin, value[:, 128:]], 1)


class Columns:
    def __init__(self, array, unit, j):
        self.array, self.unit, self.j = array, unit, j
        self.shape = array.shape[:-1] + (unit,)
        self.dtype = array.dtype
        self.size = array.size // array.shape[-1] * unit


def columns(array, unit, first, last):
    return [Columns(array, unit, j) for j in range(first, last)]


def call(kernel, outs, operands, flops, scratch=(), scalar=None):
    in_specs, arrays = [], []
    if scalar is not None:
        in_specs.append(pl.BlockSpec(memory_space=pltpu.SMEM))
        arrays.append(scalar.reshape(1).astype(jnp.int32))
    for operand in operands:
        if isinstance(operand, Columns):
            lead = (0,) * (len(operand.shape) - 1)
            in_specs.append(pl.BlockSpec(operand.shape, lambda i, lead=lead, j=operand.j: lead + (j,)))
            arrays.append(operand.array)
        else:
            zero = (0,) * len(operand.shape)
            in_specs.append(pl.BlockSpec(operand.shape, lambda i, zero=zero: zero))
            arrays.append(operand)
    out_specs = [pl.BlockSpec(o.shape, lambda i, zero=(0,) * len(o.shape): zero) for o in outs]
    return pl.pallas_call(
        kernel,
        grid=(1,),
        out_shape=outs,
        in_specs=in_specs,
        out_specs=out_specs,
        scratch_shapes=list(scratch),
        compiler_params=pltpu.CompilerParams(vmem_limit_bytes=VMEM_LIMIT),
        cost_estimate=pl.CostEstimate(flops=0, bytes_accessed=0, transcendentals=0),
    )(*arrays)


def kept_block(p, count, core):
    half = count // 2
    return 2 * (p % half) + (core if p < half else 1 - core)


def kept_difference(p, count):
    half = count // 2
    return 2 * (p % half) + p // half


def at(index, size):
    return pl.ds(pl.multiple_of(index * size, size), size)


def shaped(shape, dtype):
    return jax.ShapeDtypeStruct(shape, dtype)


def attention_kernel(x_ref, row_ref, key_ref, cos_ref, sin_ref, out_ref, dk_ref, dv_ref):
    length = x_ref.shape[0]
    hd = HEAD_DIM
    tile = min(256, length)
    keys = x_ref[:, hd : 2 * hd]
    values = x_ref[:, 2 * hd : 3 * hd]
    key_place = key_ref[0:1, :]
    for step in range(length // tile):
        rows = slice(step * tile, (step + 1) * tile)
        query = x_ref[rows, 0:hd]
        grad = x_ref[rows, 3 * hd : 4 * hd]
        place = row_ref[rows, 0:1]
        first = row_ref[rows, 1:2]
        allowed = (key_place <= place) & (key_place >= first)
        scores = jnp.where(allowed, dot_t(query, keys) * SCALE, LARGE_NEGATIVE)
        top = jnp.max(scores, 1, keepdims=True)
        weights = jnp.exp(scores - top)
        probs = weights * (1.0 / jnp.sum(weights, 1, keepdims=True))
        probs_b = probs.astype(bf16)
        attended = dot(probs_b, values).astype(bf16)
        out_ref[rows, 0:hd] = attended
        delta = jnp.sum(grad.astype(f32) * attended.astype(f32), 1, keepdims=True)
        d_probs = dot_t(grad, values)
        d_scores = (probs * (d_probs - delta) * SCALE).astype(bf16)
        d_query = dot(d_scores, keys)
        out_ref[rows, hd : 2 * hd] = turn(d_query, cos_ref[rows, :], sin_ref[rows, :]).astype(bf16)
        dk = t_dot(d_scores, query)
        dv = t_dot(probs_b, grad)
        if step == 0:
            dk_ref[...] = dk
            dv_ref[...] = dv
        else:
            dk_ref[...] += dk
            dv_ref[...] += dv
    for step in range(length // tile):
        rows = slice(step * tile, (step + 1) * tile)
        out_ref[rows, 2 * hd : 3 * hd] = turn(dk_ref[rows, :], cos_ref[rows, :], sin_ref[rows, :]).astype(bf16)
        out_ref[rows, 3 * hd : 4 * hd] = dv_ref[rows, :].astype(bf16)


def attention_tables(places, cut):
    cos_table, sin_table = rotary_tables(places, -1.0)
    return jnp.stack([places, jnp.where(places >= cut, cut, 0)], 1), places[None, :], cos_table, sin_table


def attention(packed, *tables):
    length = packed.shape[0]
    scratch = [pltpu.VMEM((length, HEAD_DIM), f32), pltpu.VMEM((length, HEAD_DIM), f32)]
    outs = [shaped((length, 4 * HEAD_DIM), bf16)]
    return call(attention_kernel, outs, (packed, *tables), 12 * length * length * HEAD_DIM, scratch)[0]


def project(acts, gain, shift_by, held, bias, cos, sin, part, tokens, index):
    rows, width = acts.shape[0], acts.shape[1] // 2
    count, unit = held.shape[0], held.shape[2] // 8
    seqs = rows // tokens
    hd = HEAD_DIM
    heads = unit // hd
    pieces = width // unit
    size = part // pieces

    def kernel(*refs):
        index_ref, acts_ref, gain_ref, shift_ref, bias_ref, cos_ref, sin_ref = refs[:7]
        w_refs, dense_in_ref = refs[7:10], refs[10]
        send_ref, h_ref, dense_ref = refs[11:]
        core = index_ref[0] & 1
        for p in range(count):
            for j in range(pieces):
                block = dense_in_ref[p, j * size : (j + 1) * size, :]
                dense_ref[p * size : (p + 1) * size, j * unit : (j + 1) * unit] = block
            cols = at(kept_block(p, count, core), part)
            h = acts_ref[:, cols].astype(f32) * gain_ref[0:1, cols] + shift_ref[0:1, cols]
            h_ref[:, p * part : (p + 1) * part] = h.astype(bf16)
        for head in range(heads):
            for piece in range(3):
                start = (head * 3 + piece) * hd
                total = jnp.broadcast_to(bias_ref[0:1, start : start + hd], (rows, hd))
                w_ref, start = w_refs[start // unit], start % unit
                for p in range(count):
                    block = w_ref[kept_block(p, count, core), :part, start : start + hd]
                    total = total + dot(h_ref[:, p * part : (p + 1) * part], block)
                if piece < 2:
                    total = turn(total, cos_ref[...], sin_ref[...])
                send_ref[:, head, :, piece * hd : (piece + 1) * hd] = total.astype(bf16).reshape(seqs, tokens, hd)
            d_att = dot_t(acts_ref[:, width:], dense_ref[head * hd : (head + 1) * hd, :])
            send_ref[:, head, :, 3 * hd :] = d_att.astype(bf16).reshape(seqs, tokens, hd)

    outs = [
        shaped((seqs, heads, tokens, 4 * hd), bf16),
        shaped((rows, width), bf16),
        shaped((unit, width), bf16),
    ]
    operands = [acts, gain[None], shift_by[None], bias[None], cos, sin]
    operands += columns(held, unit, 0, 4)
    return call(kernel, outs, operands, 8 * rows * width * unit, scalar=index)


def feed_forward(acts, gain, shift_by, held, bias, down_blocks, part, index):
    rows, width = acts.shape[0], acts.shape[1] // 2
    count, unit = held.shape[0], held.shape[2] // 8
    size = down_blocks[0].shape[0]
    hidden_n = 4 * unit
    tile = 256

    def kernel(*refs):
        index_ref, acts_ref, gain_ref, shift_ref, bias_ref = refs[:5]
        up_refs = refs[5:9]
        down_refs = refs[9 : 9 + count]
        h_ref, hidden_ref, d_pre_ref, out_ref, sum_ref, down_ref = refs[9 + count :]
        core = index_ref[0] & 1
        for p in range(count):
            down_ref[at(index_ref[0] ^ kept_difference(p, count), size), :] = down_refs[p][...]
            cols = at(kept_block(p, count, core), part)
            h = acts_ref[:, cols].astype(f32) * gain_ref[0:1, cols] + shift_ref[0:1, cols]
            h_ref[:, p * part : (p + 1) * part] = h.astype(bf16)
        for step in range(hidden_n // tile):
            cols = slice(step * tile, (step + 1) * tile)
            up_ref, start = up_refs[step * tile // unit], step * tile % unit
            pre = jnp.broadcast_to(bias_ref[0:1, cols], (rows, tile))
            for p in range(count):
                block = up_ref[kept_block(p, count, core), :part, start : start + tile]
                pre = pre + dot(h_ref[:, p * part : (p + 1) * part], block)
            activated, slope = gelu_parts(pre)
            hidden_ref[:, cols] = activated.astype(bf16)
            d_pre = dot_t(acts_ref[:, width:], down_ref[cols, :]) * slope
            sum_ref[0:1, cols] = jnp.sum(d_pre, 0, keepdims=True)
            d_pre_ref[:, cols] = d_pre.astype(bf16)
        for step in range(width // 256):
            cols = slice(step * 256, (step + 1) * 256)
            out_ref[:, cols] = dot(hidden_ref[...], down_ref[:, cols])

    outs = [
        shaped((rows, width), bf16),
        shaped((rows, hidden_n), bf16),
        shaped((rows, hidden_n), bf16),
        shaped((rows, width), f32),
        shaped((1, hidden_n), f32),
    ]
    operands = [acts, gain[None], shift_by[None], bias[None]] + columns(held, unit, 4, 8) + list(down_blocks)
    scratch = [pltpu.VMEM((hidden_n, width), bf16)]
    return call(kernel, outs, operands, 6 * rows * width * hidden_n, scratch, scalar=index)


def input_terms(d_out, held, first, acts, gain, part, e_before=None):
    rows, width = acts.shape[0], acts.shape[1] // 2
    count, unit = held.shape[0], held.shape[2] // 8
    units = d_out.shape[1] // unit

    def kernel(*refs):
        d_out_ref, acts_ref, gain_ref = refs[:3]
        w_refs = refs[3 : 3 + units]
        e_ref, sum_ref = refs[-2:]
        for p in range(count):
            cols = slice(p * part, (p + 1) * part)
            d_h = dot_t(d_out_ref[:, :unit], w_refs[0][p, :part, :])
            for j in range(1, units):
                d_h = d_h + dot_t(d_out_ref[:, j * unit : (j + 1) * unit], w_refs[j][p, :part, :])
            sum_ref[0:1, cols] = jnp.sum(d_h * acts_ref[:, cols].astype(f32), 0, keepdims=True)
            sum_ref[1:2, cols] = jnp.sum(d_h, 0, keepdims=True)
            e = d_h * gain_ref[0:1, cols]
            if e_before is not None:
                e = e + refs[3 + units][:, cols]
            e_ref[:, cols] = e.astype(e_ref.dtype)

    outs = [shaped((rows, width), f32 if e_before is None else bf16), shaped((2, width), f32)]
    operands = [d_out, acts, gain[None]] + columns(held, unit, first, first + units)
    if e_before is not None:
        operands.append(e_before)
    return call(kernel, outs, operands, 2 * rows * width * d_out.shape[1])


def split_columns(w_qkv, w_up, wsh, ctx):
    rows = w_qkv.shape[0]
    width = w_qkv.shape[1] // 3
    hd = HEAD_DIM
    heads = HEADS // wsh
    fl = w_up.shape[1] // (ctx * wsh)

    def kernel(qkv_ref, up_ref, out_ref):
        for z in range(wsh):
            for head in range(heads):
                for piece in range(3):
                    start = piece * width + (z * heads + head) * hd
                    to = (head * 3 + piece) * hd
                    out_ref[z, :, to : to + hd] = qkv_ref[:, start : start + hd]
            out_ref[z, :, 3 * heads * hd :] = jnp.concatenate(
                [up_ref[:, (c * wsh + z) * fl : (c * wsh + z + 1) * fl] for c in range(ctx)], 1
            )

    outs = [shaped((wsh, rows, 3 * heads * hd + ctx * fl), bf16)]
    return call(kernel, outs, (w_qkv, w_up), 0)[0]


def join_qkv(parts, columns):
    wsh, rows, _ = parts.shape
    hd = HEAD_DIM
    heads = HEADS // wsh

    def kernel(in_ref, out_ref):
        for z in range(wsh):
            for head in range(heads):
                for piece in range(3):
                    to = piece * HEADS * hd + (z * heads + head) * hd
                    start = (head * 3 + piece) * hd
                    out_ref[:, to : to + hd] = in_ref[z, :, start : start + hd].astype(f32)

    return call(kernel, [shaped((rows, wsh * columns), f32)], (parts,), 0)[0]


def join_up(parts, first, ctx):
    wsh, rows, columns = parts.shape
    fl = (columns - first) // ctx

    def kernel(in_ref, out_ref):
        for c in range(ctx):
            start = first + c * fl
            out_ref[:, c * wsh * fl : (c + 1) * wsh * fl] = jnp.concatenate(
                [in_ref[z, :, start : start + fl].astype(f32) for z in range(wsh)], 1
            )

    return call(kernel, [shaped((rows, wsh * (columns - first)), f32)], (parts,), 0)[0]


def unpack(result):
    seqs, heads, tokens, _ = result.shape
    hd = HEAD_DIM
    rows = seqs * tokens

    def kernel(in_ref, att_ref, proj_ref, sum_ref):
        for head in range(heads):
            value = in_ref[:, head].reshape(rows, 4 * hd)
            att_ref[:, head * hd : (head + 1) * hd] = value[:, :hd]
            proj_ref[:, head * 3 * hd : (head + 1) * 3 * hd] = value[:, hd:]
            sum_ref[0:1, head * 3 * hd : (head + 1) * 3 * hd] = jnp.sum(value[:, hd:].astype(f32), 0, keepdims=True)

    outs = [
        shaped((rows, heads * hd), bf16),
        shaped((rows, heads * 3 * hd), bf16),
        shaped((1, heads * 3 * hd), f32),
    ]
    return call(kernel, outs, (result,), 0)


CTX = ("chip", "core")


def after(value, *others):
    return lax.optimization_barrier((value,) + others)[0]


def hop(value):
    return lax.ppermute(value, "core", [(0, 1), (1, 0)])


def exchange(value, axis):
    return lax.all_to_all(value, axis, 0, 0, tiled=True)


def chip_hop(value, k):
    n = lax.axis_size("chip")
    return lax.ppermute(value, "chip", [(i, i ^ k) for i in range(n)])


def shift(value, step):
    n = lax.axis_size("wsh")
    return lax.ppermute(value, "wsh", [(i, (i + step) % n) for i in range(n)])


def chip_blocks(block):
    return [block] + [chip_hop(block, k) for k in range(1, lax.axis_size("chip"))]


def with_other_core(own):
    return list(own) + [hop(value) for value in own]


def sum_arrived(value):
    return jnp.sum(value.astype(f32), 0).astype(bf16)


def over_cores_send(value):
    return hop(lax.dynamic_index_in_dim(value, 1 - lax.axis_index("core"), 1, False))


def over_cores_add(value, away):
    kept = lax.dynamic_index_in_dim(value, lax.axis_index("core"), 1, False)
    return (kept.astype(f32) + away.astype(f32)).astype(bf16)


def hop_terms(terms):
    return [chip_hop(term, k) for k, term in enumerate(terms) if k]


def sum_terms(own, arrived):
    total = own.astype(f32)
    for term in arrived:
        total = total + term.astype(f32)
    return total.astype(bf16)


def body(
    inputs,
    cotangent,
    block_order,
    doc_cut,
    w_qkv,
    b_qkv,
    w_dense,
    b_dense,
    w_up,
    b_up,
    w_down,
    b_down,
    gain_attn,
    shift_attn,
    gain_mlp,
    shift_mlp,
):
    both = CTX + ("wsh",)
    C = lax.axis_size(CTX)
    W = lax.axis_size("wsh")
    core = lax.axis_index("core")
    c = lax.axis_index(CTX)
    z = lax.axis_index("wsh")
    T, D = inputs.shape[1:]
    DL = w_qkv.shape[0]
    FL = w_down.shape[0]
    E = D // W
    HL = HEADS // W
    PAIRS = W * HL
    R = C // PAIRS
    PART = D // C
    x = inputs[0]
    cot = cotangent[0]

    moves = [(i, (i % C) * W + i // C) for i in range(C * W)]
    back_moves = [(j, i) for i, j in moves]
    own_down = chip_blocks(w_down)
    moved_dense = lax.ppermute(w_dense, both, moves)

    centre = x - jnp.mean(x, -1, keepdims=True)
    inv_std = lax.rsqrt(jnp.mean(centre * centre, -1, keepdims=True) + NORM_EPS)
    normed = centre * inv_std
    acts = jnp.concatenate([normed.astype(bf16), cot.astype(bf16)], 1)
    cut = doc_cut[0]
    ints = jnp.concatenate([block_order[0], (cut // 16)[None], (cut % 16)[None]]).astype(bf16)
    small = [b_qkv, b_dense, b_up, b_down, gain_attn, shift_attn, gain_mlp, shift_mlp, ints]
    sizes = [a.shape[0] for a in small]
    starts = [sum(sizes[:i]) for i in range(len(sizes))]
    rider = jnp.concatenate(small + [jnp.zeros((3 * E - sum(sizes),), bf16)])
    turned = exchange(split_columns(w_qkv, w_up, W, C), "wsh")
    rider = jnp.broadcast_to(rider, (16, 3 * E))
    riders = jnp.broadcast_to(rider[:1], (16, 3 * E))
    for k in range(1, W):
        riders = lax.dynamic_update_slice_in_dim(riders, shift(rider, k)[:1], (z - k) % W, 0)
    riders = lax.dynamic_update_slice_in_dim(riders, rider[:1], z, 0)
    turned, acts, riders, moved_dense, *own_down = lax.optimization_barrier((turned, acts, riders, moved_dense, *own_down))
    dense_part = moved_dense.reshape(DL, W, E).transpose(1, 0, 2).reshape(W * DL, E)
    turned = turned.reshape(W * DL, 7 * E)
    held = jnp.concatenate([turned[:, : 3 * E], dense_part, turned[:, 3 * E :]], 1)
    held = jnp.concatenate([held, jnp.pad(riders, ((0, 0), (0, 5 * E)))], 0)
    held = lax.all_gather(held[None], CTX, axis=0, tiled=True)
    acts_all = jnp.zeros((W, T, 2 * D), bf16)
    acts_all = lax.dynamic_update_slice_in_dim(acts_all, acts[None], z, 0)
    for k in range(1, W):
        acts_all = lax.dynamic_update_slice_in_dim(acts_all, shift(acts, k)[None], (z - k) % W, 0)
    acts = acts_all.reshape(W * T, 2 * D)
    g = acts[:, D:]
    blocks_down = with_other_core(own_down)
    held, acts, *blocks_down = lax.optimization_barrier((held, acts, *blocks_down))
    pack = held[:, W * DL : W * DL + W, : 3 * E]
    pieces = [pack[:, :, s : s + n].astype(f32) for s, n in zip(starts, sizes)]
    bias_qkv, bias_dense, bias_up, bias_down, ga, sa, gm, sm = [p.reshape(-1) for p in pieces[:8]]
    info = pieces[-1][0].astype(jnp.int32)
    orders = info[:, :C]
    cuts = info[:, C] * 16 + info[:, C + 1]
    bias_qkv = lax.dynamic_index_in_dim(bias_qkv.reshape(3, W, HL, HEAD_DIM), z, 1, False).transpose(1, 0, 2).reshape(3 * E)
    bias_up = lax.dynamic_index_in_dim(pieces[2], z, 1, False).reshape(C * FL)

    own_places = block_places(lax.dynamic_index_in_dim(orders, c, 1, False), C, T).reshape(-1)
    own_cos, own_sin = rotary_tables(own_places, 1.0)
    seq = c // R // HL
    seq_order = lax.dynamic_index_in_dim(orders, seq, 0, False)
    seq_cut = lax.dynamic_index_in_dim(cuts, seq, 0, False)
    tables = attention_tables(block_places(seq_order, C, T).reshape(-1), seq_cut)
    send, h_attn, full_dense = project(acts, ga, sa, held, bias_qkv, own_cos, own_sin, PART, T, c)
    send = send.reshape(PAIRS, T, 4 * HEAD_DIM)
    if R > 1:
        send = jnp.repeat(send, R, 0)
    packed = exchange(send, CTX).reshape(C * T, 4 * HEAD_DIM)

    h_mlp, hidden, d_pre, out_mlp, sum_pre = feed_forward(
        after(acts, send, *tables), gm, sm, held, bias_up, blocks_down, PART, c
    )
    result = attention(after(packed, d_pre), *tables)

    h_late = after(h_mlp, result)
    result = exchange(result.reshape(C, T, 4 * HEAD_DIM), CTX)
    away_up = hop(t_dot(h_late[:, D // 2 :], d_pre).astype(bf16))
    gw_down = t_dot(after(hidden, away_up), g).astype(bf16)
    kept_up = (t_dot(h_late[:, : D // 2], d_pre) + away_up.astype(f32)).astype(bf16)
    result = after(result, gw_down, kept_up)
    arrived_up = exchange(after(kept_up, result).reshape(C // 2, PART, C * FL), "chip")
    if R > 1:
        result = result.reshape(PAIRS, R, T, 4 * HEAD_DIM)[:, 0]
    attended, d_proj, sum_proj = unpack(result.reshape(W, HL, T, 4 * HEAD_DIM))
    away_qkv = t_dot(h_attn[:, D // 2 :], d_proj).astype(bf16)
    out_part = (out_mlp + dot(after(attended, away_qkv), full_dense)).astype(bf16)
    away_here = hop(away_qkv)
    out_sum = lax.psum_scatter(out_part.reshape(W * T, D), "wsh", scatter_dimension=0, tiled=True)
    kept_qkv = (t_dot(after(h_attn, out_part)[:, : D // 2], d_proj) + away_here.astype(f32)).astype(bf16)
    e_mlp, sums_mlp = input_terms(after(d_pre, kept_qkv), held, 4, acts, gm, PART)
    e_part, sums_attn = input_terms(d_proj, held, 0, acts, ga, PART, e_mlp)
    e_part, out_sum = lax.optimization_barrier((e_part, out_sum))
    arrived_up = after(arrived_up, e_part)
    arrived_qkv = exchange(after(kept_qkv, arrived_up).reshape(C // 2, PART, 3 * E), "chip")
    e_sum = lax.psum_scatter(e_part, "wsh", scatter_dimension=0, tiled=True)

    gw_dense = t_dot(after(attended, e_part), g).astype(bf16).reshape(C // 2, 2, DL, D)
    kept_dense = over_cores_add(gw_dense, over_cores_send(gw_dense))
    own_up = sum_arrived(arrived_up)
    arrived_qkv = after(arrived_qkv, own_up, kept_dense)
    own_grads = jnp.concatenate([sum_arrived(arrived_qkv), own_up], 1)
    back = exchange(own_grads.reshape(W, DL, 7 * E), "wsh")
    grad_down = lax.psum_scatter(after(gw_down, arrived_qkv), CTX, scatter_dimension=0, tiled=True).astype(f32)
    terms = [lax.dynamic_index_in_dim(kept_dense, lax.axis_index("chip") ^ k, 0, False) for k in range(C // 2)]
    grad_dense = lax.ppermute(sum_terms(terms[0], hop_terms(terms)), both, back_moves).astype(f32)

    output = x + out_sum.astype(f32) + (bias_dense + bias_down)
    e = e_sum.astype(f32)
    input_gradient = (
        cot + (e - jnp.mean(e, -1, keepdims=True) - normed * jnp.mean(e * normed, -1, keepdims=True)) * inv_std
    )
    grad_qkv = join_qkv(back, 3 * E)
    grad_up = join_up(back, 3 * E, C)

    sum_proj = sum_proj.reshape(HL, 3, HEAD_DIM).transpose(1, 0, 2).reshape(3, 1, E)
    gb_qkv = lax.dynamic_update_slice_in_dim(jnp.zeros((3, W, E), f32), sum_proj, z, 1).reshape(C * W, -1)
    gb_up = lax.dynamic_update_slice_in_dim(jnp.zeros((C, W, FL), f32), sum_pre.reshape(C, 1, FL), z, 1)
    gb_up = gb_up.reshape(C * W, FL)
    by_width = jnp.concatenate([sums_attn, sums_mlp, jnp.sum(cot, 0, keepdims=True)], 0)
    by_width = by_width.reshape(5, C * W, DL).transpose(1, 0, 2).reshape(C * W, 5 * DL)
    vectors = jnp.concatenate([gb_up, gb_qkv, by_width], 1)
    summed = jnp.sum(exchange(after(vectors, back), both), 0)
    n_up, n_qkv = gb_up.shape[1], gb_qkv.shape[1]
    gb_up, gb_qkv = summed[:n_up], summed[n_up : n_up + n_qkv]
    g_ga, g_sa, g_gm, g_sm, gb_dense = [
        summed[n_up + n_qkv + i * DL : n_up + n_qkv + (i + 1) * DL] for i in range(5)
    ]
    return (
        output[None],
        input_gradient[None],
        grad_qkv,
        gb_qkv,
        grad_dense,
        gb_dense,
        grad_up,
        gb_up,
        grad_down,
        gb_dense,
        g_ga,
        g_sa,
        g_gm,
        g_sm,
    )


def solution(mesh):
    ctx, wsh = mesh.shape["ctx"], mesh.shape["wsh"]
    split = Mesh(mesh.devices.reshape(ctx // 2, 2, wsh), CTX + ("wsh",))
    tokens = P("wsh", CTX, None)
    matrix = P(CTX + ("wsh",), None)
    vector = P(CTX + ("wsh",))
    pairs = (matrix, vector) * 4
    return jax.shard_map(
        body,
        mesh=split,
        in_specs=(tokens, tokens, P("wsh", None), P("wsh")) + pairs + (vector,) * 4,
        out_specs=(tokens, tokens) + pairs + (vector,) * 4,
        check_vma=False,
    )
```

```python
import jax
import jax.numpy as jnp
from jax import lax
from jax.experimental import pallas as pl
from jax.experimental.pallas import tpu as pltpu
from jax.sharding import Mesh
from jax.sharding import PartitionSpec as P

HEADS = 8
HEAD_DIM = 256
ROT_DIM = 64
HALF = ROT_DIM // 2
NORM_EPS = 1e-05
LARGE_NEGATIVE = -1e30
SCALE = HEAD_DIM ** (-0.5)
f32 = jnp.float32
bf16 = jnp.bfloat16


def dot(a, b):
    return jnp.dot(a, b, preferred_element_type=f32)


def dot_t(a, b):
    return lax.dot_general(a, b, (((1,), (1,)), ((), ())), preferred_element_type=f32)


def t_dot(a, b):
    return lax.dot_general(a, b, (((0,), (0,)), ((), ())), preferred_element_type=f32)


def angles_of(places):
    frequency = jnp.power(10000.0, -2.0 * jnp.arange(HALF).astype(f32) / ROT_DIM)
    return places.astype(f32)[..., None] * frequency


def gelu_parts(pre_act):
    normal_cdf = 0.5 * (1.0 + lax.erf(pre_act * 0.7071067811865476))
    density = jnp.exp(-0.5 * pre_act * pre_act) * 0.3989422804014327
    return (pre_act * normal_cdf, normal_cdf + pre_act * density)


def block_places(order, ctx_count, tok_rows):
    half = tok_rows // 2
    within = jnp.arange(tok_rows, dtype=jnp.int32)
    first = order[..., None]
    block = jnp.where(within < half, first, 2 * ctx_count - 1 - first)
    return block * half + within % half


VMEM_LIMIT = 56 * 2**20


def rotary_tables(places, direction):
    angle = angles_of(places)
    cos, sin = jnp.cos(angle), jnp.sin(angle) * direction
    rest = 128 - ROT_DIM
    ones = jnp.ones((places.shape[0], rest), f32)
    return jnp.concatenate([cos, cos, ones], 1), jnp.concatenate([-sin, sin, 0.0 * ones], 1)


def turn(value, cos, sin):
    low = value[:, :128]
    lane = lax.broadcasted_iota(jnp.int32, low.shape, 1)
    other = jnp.where(lane < HALF, pltpu.roll(low, 128 - HALF, 1), pltpu.roll(low, HALF, 1))
    return jnp.concatenate([low * cos + other * sin, value[:, 128:]], 1)


class Columns:
    def __init__(self, array, unit, j):
        self.array, self.unit, self.j = array, unit, j
        self.shape = array.shape[:-1] + (unit,)
        self.dtype = array.dtype
        self.size = array.size // array.shape[-1] * unit


def columns(array, unit, first, last):
    return [Columns(array, unit, j) for j in range(first, last)]


def call(kernel, outs, operands, flops, scratch=(), scalar=None):
    in_specs, arrays = [], []
    if scalar is not None:
        in_specs.append(pl.BlockSpec(memory_space=pltpu.SMEM))
        arrays.append(scalar.reshape(1).astype(jnp.int32))
    for operand in operands:
        if isinstance(operand, Columns):
            lead = (0,) * (len(operand.shape) - 1)
            in_specs.append(pl.BlockSpec(operand.shape, lambda i, lead=lead, j=operand.j: lead + (j,)))
            arrays.append(operand.array)
        else:
            zero = (0,) * len(operand.shape)
            in_specs.append(pl.BlockSpec(operand.shape, lambda i, zero=zero: zero))
            arrays.append(operand)
    out_specs = [pl.BlockSpec(o.shape, lambda i, zero=(0,) * len(o.shape): zero) for o in outs]
    return pl.pallas_call(
        kernel,
        grid=(1,),
        out_shape=outs,
        in_specs=in_specs,
        out_specs=out_specs,
        scratch_shapes=list(scratch),
        compiler_params=pltpu.CompilerParams(vmem_limit_bytes=VMEM_LIMIT),
        cost_estimate=pl.CostEstimate(flops=0, bytes_accessed=0, transcendentals=0),
    )(*arrays)


def kept_block(p, count, core):
    half = count // 2
    return 2 * (p % half) + (core if p < half else 1 - core)


def kept_difference(p, count):
    half = count // 2
    return 2 * (p % half) + p // half


def at(index, size):
    return pl.ds(pl.multiple_of(index * size, size), size)


def shaped(shape, dtype):
    return jax.ShapeDtypeStruct(shape, dtype)


def attention_kernel(x_ref, row_ref, key_ref, cos_ref, sin_ref, out_ref, dk_ref, dv_ref):
    length = x_ref.shape[0]
    hd = HEAD_DIM
    tile = min(256, length)
    keys = x_ref[:, hd : 2 * hd]
    values = x_ref[:, 2 * hd : 3 * hd]
    key_place = key_ref[0:1, :]
    for step in range(length // tile):
        rows = slice(step * tile, (step + 1) * tile)
        query = x_ref[rows, 0:hd]
        grad = x_ref[rows, 3 * hd : 4 * hd]
        place = row_ref[rows, 0:1]
        first = row_ref[rows, 1:2]
        allowed = (key_place <= place) & (key_place >= first)
        scores = jnp.where(allowed, dot_t(query, keys) * SCALE, LARGE_NEGATIVE)
        top = jnp.max(scores, 1, keepdims=True)
        weights = jnp.exp(scores - top)
        probs = weights * (1.0 / jnp.sum(weights, 1, keepdims=True))
        probs_b = probs.astype(bf16)
        attended = dot(probs_b, values).astype(bf16)
        out_ref[rows, 0:hd] = attended
        delta = jnp.sum(grad.astype(f32) * attended.astype(f32), 1, keepdims=True)
        d_probs = dot_t(grad, values)
        d_scores = (probs * (d_probs - delta) * SCALE).astype(bf16)
        d_query = dot(d_scores, keys)
        out_ref[rows, hd : 2 * hd] = turn(d_query, cos_ref[rows, :], sin_ref[rows, :]).astype(bf16)
        dk = t_dot(d_scores, query)
        dv = t_dot(probs_b, grad)
        if step == 0:
            dk_ref[...] = dk
            dv_ref[...] = dv
        else:
            dk_ref[...] += dk
            dv_ref[...] += dv
    for step in range(length // tile):
        rows = slice(step * tile, (step + 1) * tile)
        out_ref[rows, 2 * hd : 3 * hd] = turn(dk_ref[rows, :], cos_ref[rows, :], sin_ref[rows, :]).astype(bf16)
        out_ref[rows, 3 * hd : 4 * hd] = dv_ref[rows, :].astype(bf16)


def attention_tables(places, cut):
    cos_table, sin_table = rotary_tables(places, -1.0)
    return jnp.stack([places, jnp.where(places >= cut, cut, 0)], 1), places[None, :], cos_table, sin_table


def attention(packed, *tables):
    length = packed.shape[0]
    scratch = [pltpu.VMEM((length, HEAD_DIM), f32), pltpu.VMEM((length, HEAD_DIM), f32)]
    outs = [shaped((length, 4 * HEAD_DIM), bf16)]
    return call(attention_kernel, outs, (packed, *tables), 12 * length * length * HEAD_DIM, scratch)[0]


def project(acts, gain, shift_by, held, bias, cos, sin, part, tokens, index):
    rows, width = acts.shape[0], acts.shape[1] // 2
    count, unit = held.shape[0], held.shape[2] // 8
    seqs = rows // tokens
    hd = HEAD_DIM
    heads = unit // hd
    pieces = width // unit
    size = part // pieces

    def kernel(*refs):
        index_ref, acts_ref, gain_ref, shift_ref, bias_ref, cos_ref, sin_ref = refs[:7]
        w_refs, dense_in_ref = refs[7:10], refs[10]
        send_ref, h_ref, dense_ref = refs[11:]
        core = index_ref[0] & 1
        for p in range(count):
            for j in range(pieces):
                block = dense_in_ref[p, j * size : (j + 1) * size, :]
                dense_ref[p * size : (p + 1) * size, j * unit : (j + 1) * unit] = block
            cols = at(kept_block(p, count, core), part)
            h = acts_ref[:, cols].astype(f32) * gain_ref[0:1, cols] + shift_ref[0:1, cols]
            h_ref[:, p * part : (p + 1) * part] = h.astype(bf16)
        for head in range(heads):
            for piece in range(3):
                start = (head * 3 + piece) * hd
                total = jnp.broadcast_to(bias_ref[0:1, start : start + hd], (rows, hd))
                w_ref, start = w_refs[start // unit], start % unit
                for p in range(count):
                    block = w_ref[kept_block(p, count, core), :part, start : start + hd]
                    total = total + dot(h_ref[:, p * part : (p + 1) * part], block)
                if piece < 2:
                    total = turn(total, cos_ref[...], sin_ref[...])
                send_ref[:, head, :, piece * hd : (piece + 1) * hd] = total.astype(bf16).reshape(seqs, tokens, hd)
            d_att = dot_t(acts_ref[:, width:], dense_ref[head * hd : (head + 1) * hd, :])
            send_ref[:, head, :, 3 * hd :] = d_att.astype(bf16).reshape(seqs, tokens, hd)

    outs = [
        shaped((seqs, heads, tokens, 4 * hd), bf16),
        shaped((rows, width), bf16),
        shaped((unit, width), bf16),
    ]
    operands = [acts, gain[None], shift_by[None], bias[None], cos, sin]
    operands += columns(held, unit, 0, 4)
    return call(kernel, outs, operands, 8 * rows * width * unit, scalar=index)


def feed_forward(acts, gain, shift_by, held, bias, down_blocks, part, index):
    rows, width = acts.shape[0], acts.shape[1] // 2
    count, unit = held.shape[0], held.shape[2] // 8
    size = down_blocks[0].shape[0]
    hidden_n = 4 * unit
    tile = 256

    def kernel(*refs):
        index_ref, acts_ref, gain_ref, shift_ref, bias_ref = refs[:5]
        up_refs = refs[5:9]
        down_refs = refs[9 : 9 + count]
        h_ref, hidden_ref, d_pre_ref, out_ref, sum_ref, down_ref = refs[9 + count :]
        core = index_ref[0] & 1
        for p in range(count):
            down_ref[at(index_ref[0] ^ kept_difference(p, count), size), :] = down_refs[p][...]
            cols = at(kept_block(p, count, core), part)
            h = acts_ref[:, cols].astype(f32) * gain_ref[0:1, cols] + shift_ref[0:1, cols]
            h_ref[:, p * part : (p + 1) * part] = h.astype(bf16)
        for step in range(hidden_n // tile):
            cols = slice(step * tile, (step + 1) * tile)
            up_ref, start = up_refs[step * tile // unit], step * tile % unit
            pre = jnp.broadcast_to(bias_ref[0:1, cols], (rows, tile))
            for p in range(count):
                block = up_ref[kept_block(p, count, core), :part, start : start + tile]
                pre = pre + dot(h_ref[:, p * part : (p + 1) * part], block)
            activated, slope = gelu_parts(pre)
            hidden_ref[:, cols] = activated.astype(bf16)
            d_pre = dot_t(acts_ref[:, width:], down_ref[cols, :]) * slope
            sum_ref[0:1, cols] = jnp.sum(d_pre, 0, keepdims=True)
            d_pre_ref[:, cols] = d_pre.astype(bf16)
        for step in range(width // 256):
            cols = slice(step * 256, (step + 1) * 256)
            out_ref[:, cols] = dot(hidden_ref[...], down_ref[:, cols])

    outs = [
        shaped((rows, width), bf16),
        shaped((rows, hidden_n), bf16),
        shaped((rows, hidden_n), bf16),
        shaped((rows, width), f32),
        shaped((1, hidden_n), f32),
    ]
    operands = [acts, gain[None], shift_by[None], bias[None]] + columns(held, unit, 4, 8) + list(down_blocks)
    scratch = [pltpu.VMEM((hidden_n, width), bf16)]
    return call(kernel, outs, operands, 6 * rows * width * hidden_n, scratch, scalar=index)


def input_terms(d_out, held, first, acts, gain, part, e_before=None):
    rows, width = acts.shape[0], acts.shape[1] // 2
    count, unit = held.shape[0], held.shape[2] // 8
    units = d_out.shape[1] // unit

    def kernel(*refs):
        d_out_ref, acts_ref, gain_ref = refs[:3]
        w_refs = refs[3 : 3 + units]
        e_ref, sum_ref = refs[-2:]
        for p in range(count):
            cols = slice(p * part, (p + 1) * part)
            d_h = dot_t(d_out_ref[:, :unit], w_refs[0][p, :part, :])
            for j in range(1, units):
                d_h = d_h + dot_t(d_out_ref[:, j * unit : (j + 1) * unit], w_refs[j][p, :part, :])
            sum_ref[0:1, cols] = jnp.sum(d_h * acts_ref[:, cols].astype(f32), 0, keepdims=True)
            sum_ref[1:2, cols] = jnp.sum(d_h, 0, keepdims=True)
            e = d_h * gain_ref[0:1, cols]
            if e_before is not None:
                e = e + refs[3 + units][:, cols]
            e_ref[:, cols] = e.astype(e_ref.dtype)

    outs = [shaped((rows, width), f32 if e_before is None else bf16), shaped((2, width), f32)]
    operands = [d_out, acts, gain[None]] + columns(held, unit, first, first + units)
    if e_before is not None:
        operands.append(e_before)
    return call(kernel, outs, operands, 2 * rows * width * d_out.shape[1])


def split_columns(w_qkv, w_up, wsh, ctx):
    rows = w_qkv.shape[0]
    width = w_qkv.shape[1] // 3
    hd = HEAD_DIM
    heads = HEADS // wsh
    fl = w_up.shape[1] // (ctx * wsh)

    def kernel(qkv_ref, up_ref, out_ref):
        for z in range(wsh):
            for head in range(heads):
                for piece in range(3):
                    start = piece * width + (z * heads + head) * hd
                    to = (head * 3 + piece) * hd
                    out_ref[z, :, to : to + hd] = qkv_ref[:, start : start + hd]
            out_ref[z, :, 3 * heads * hd :] = jnp.concatenate(
                [up_ref[:, (c * wsh + z) * fl : (c * wsh + z + 1) * fl] for c in range(ctx)], 1
            )

    outs = [shaped((wsh, rows, 3 * heads * hd + ctx * fl), bf16)]
    return call(kernel, outs, (w_qkv, w_up), 0)[0]


def join_qkv(parts, columns):
    wsh, rows, _ = parts.shape
    hd = HEAD_DIM
    heads = HEADS // wsh

    def kernel(in_ref, out_ref):
        for z in range(wsh):
            for head in range(heads):
                for piece in range(3):
                    to = piece * HEADS * hd + (z * heads + head) * hd
                    start = (head * 3 + piece) * hd
                    out_ref[:, to : to + hd] = in_ref[z, :, start : start + hd].astype(f32)

    return call(kernel, [shaped((rows, wsh * columns), f32)], (parts,), 0)[0]


def join_up(parts, first, ctx):
    wsh, rows, columns = parts.shape
    fl = (columns - first) // ctx

    def kernel(in_ref, out_ref):
        for c in range(ctx):
            start = first + c * fl
            out_ref[:, c * wsh * fl : (c + 1) * wsh * fl] = jnp.concatenate(
                [in_ref[z, :, start : start + fl].astype(f32) for z in range(wsh)], 1
            )

    return call(kernel, [shaped((rows, wsh * (columns - first)), f32)], (parts,), 0)[0]


def unpack(result, h_kept, dense, out_mlp):
    seqs, heads, tokens, _ = result.shape
    hd = HEAD_DIM
    rows, width = out_mlp.shape
    half = width // 2
    tile = 256

    def kernel(in_ref, h_ref, dense_ref, out_mlp_ref, att_ref, proj_ref, sum_ref, away_ref, out_ref):
        for head in range(heads):
            value = in_ref[:, head].reshape(rows, 4 * hd)
            att_ref[:, head * hd : (head + 1) * hd] = value[:, :hd]
            proj_ref[:, head * 3 * hd : (head + 1) * 3 * hd] = value[:, hd:]
            sum_ref[0:1, head * 3 * hd : (head + 1) * 3 * hd] = jnp.sum(value[:, hd:].astype(f32), 0, keepdims=True)
        for start in range(0, half, tile):
            away_ref[start : start + tile, :] = t_dot(h_ref[:, half + start : half + start + tile], proj_ref[...]).astype(bf16)
        for start in range(0, width, tile):
            cols = slice(start, start + tile)
            out_ref[:, cols] = (out_mlp_ref[:, cols] + dot(att_ref[...], dense_ref[:, cols])).astype(bf16)

    outs = [
        shaped((rows, heads * hd), bf16),
        shaped((rows, heads * 3 * hd), bf16),
        shaped((1, heads * 3 * hd), f32),
        shaped((half, heads * 3 * hd), bf16),
        shaped((rows, width), bf16),
    ]
    return call(kernel, outs, (result, h_kept, dense, out_mlp), 0)


def product_plus(left, right, term):
    tile = 256

    def kernel(left_ref, right_ref, term_ref, out_ref):
        for start in range(0, left.shape[1] // 2, tile):
            rows = slice(start, start + tile)
            out_ref[rows, :] = (t_dot(left_ref[:, rows], right_ref[...]) + term_ref[rows, :].astype(f32)).astype(bf16)

    return call(kernel, [shaped(term.shape, bf16)], (left, right, term), 0)[0]


def product_away(left, right):
    tile = 256
    half = left.shape[1] // 2

    def kernel(left_ref, right_ref, out_ref):
        for start in range(0, half, tile):
            value = t_dot(left_ref[:, half + start : half + start + tile], right_ref[...])
            out_ref[start : start + tile, :] = value.astype(bf16)

    return call(kernel, [shaped((half, right.shape[1]), bf16)], (left, right), 0)[0]


def product_by_core(left, acts, count, index):
    width = acts.shape[1] // 2
    size = left.shape[1] // count

    def kernel(index_ref, left_ref, acts_ref, own_ref, other_ref):
        core = index_ref[0] & 1
        for j in range(count // 2):
            for o in range(2):
                start = (2 * j + o) * size
                value = t_dot(left_ref[:, start : start + size], acts_ref[:, width:]).astype(bf16)

                @pl.when(core == o)
                def _():
                    own_ref[j] = value

                @pl.when(core != o)
                def _():
                    other_ref[j] = value

    outs = [shaped((count // 2, size, width), bf16)] * 2
    return call(kernel, outs, (left, acts), 0, scalar=index)


CTX = ("chip", "core")


def after(value, *others):
    return lax.optimization_barrier((value,) + others)[0]


def hop(value):
    return lax.ppermute(value, "core", [(0, 1), (1, 0)])


def exchange(value, axis):
    return lax.all_to_all(value, axis, 0, 0, tiled=True)


def chip_hop(value, k):
    n = lax.axis_size("chip")
    return lax.ppermute(value, "chip", [(i, i ^ k) for i in range(n)])


def shift(value, step):
    n = lax.axis_size("wsh")
    return lax.ppermute(value, "wsh", [(i, (i + step) % n) for i in range(n)])


def chip_blocks(block):
    return [block] + [chip_hop(block, k) for k in range(1, lax.axis_size("chip"))]


def with_other_core(own):
    return list(own) + [hop(value) for value in own]


def sum_arrived(value):
    return jnp.sum(value.astype(f32), 0).astype(bf16)


def over_cores_send(value):
    return hop(lax.dynamic_index_in_dim(value, 1 - lax.axis_index("core"), 1, False))


def over_cores_add(value, away):
    kept = lax.dynamic_index_in_dim(value, lax.axis_index("core"), 1, False)
    return (kept.astype(f32) + away.astype(f32)).astype(bf16)


def hop_terms(terms):
    return [chip_hop(term, k) for k, term in enumerate(terms) if k]


def sum_terms(own, arrived):
    total = own.astype(f32)
    for term in arrived:
        total = total + term.astype(f32)
    return total.astype(bf16)


def body(
    inputs,
    cotangent,
    block_order,
    doc_cut,
    w_qkv,
    b_qkv,
    w_dense,
    b_dense,
    w_up,
    b_up,
    w_down,
    b_down,
    gain_attn,
    shift_attn,
    gain_mlp,
    shift_mlp,
):
    both = CTX + ("wsh",)
    C = lax.axis_size(CTX)
    W = lax.axis_size("wsh")
    core = lax.axis_index("core")
    c = lax.axis_index(CTX)
    z = lax.axis_index("wsh")
    T, D = inputs.shape[1:]
    DL = w_qkv.shape[0]
    FL = w_down.shape[0]
    E = D // W
    HL = HEADS // W
    PAIRS = W * HL
    R = C // PAIRS
    PART = D // C
    x = inputs[0]
    cot = cotangent[0]

    moves = [(i, (i % C) * W + i // C) for i in range(C * W)]
    back_moves = [(j, i) for i, j in moves]
    own_down = chip_blocks(w_down)
    moved_dense = lax.ppermute(w_dense, both, moves)

    centre = x - jnp.mean(x, -1, keepdims=True)
    inv_std = lax.rsqrt(jnp.mean(centre * centre, -1, keepdims=True) + NORM_EPS)
    normed = centre * inv_std
    acts = jnp.concatenate([normed.astype(bf16), cot.astype(bf16)], 1)
    cut = doc_cut[0]
    ints = jnp.concatenate([block_order[0], (cut // 16)[None], (cut % 16)[None]]).astype(bf16)
    small = [b_qkv, b_dense, b_up, b_down, gain_attn, shift_attn, gain_mlp, shift_mlp, ints]
    sizes = [a.shape[0] for a in small]
    starts = [sum(sizes[:i]) for i in range(len(sizes))]
    rider = jnp.concatenate(small + [jnp.zeros((3 * E - sum(sizes),), bf16)])
    turned = exchange(split_columns(w_qkv, w_up, W, C), "wsh")
    rider = jnp.broadcast_to(rider, (16, 3 * E))
    riders = jnp.broadcast_to(rider[:1], (16, 3 * E))
    for k in range(1, W):
        riders = lax.dynamic_update_slice_in_dim(riders, shift(rider, k)[:1], (z - k) % W, 0)
    riders = lax.dynamic_update_slice_in_dim(riders, rider[:1], z, 0)
    turned, acts, riders, moved_dense, *own_down = lax.optimization_barrier((turned, acts, riders, moved_dense, *own_down))
    dense_part = moved_dense.reshape(DL, W, E).transpose(1, 0, 2).reshape(W * DL, E)
    turned = turned.reshape(W * DL, 7 * E)
    held = jnp.concatenate([turned[:, : 3 * E], dense_part, turned[:, 3 * E :]], 1)
    held = jnp.concatenate([held, jnp.pad(riders, ((0, 0), (0, 5 * E)))], 0)
    held = lax.all_gather(held[None], CTX, axis=0, tiled=True)
    info = riders[:W, starts[-1] : starts[-1] + sizes[-1]].astype(f32).astype(jnp.int32)
    orders = info[:, :C]
    cuts = info[:, C] * 16 + info[:, C + 1]
    own_places = block_places(lax.dynamic_index_in_dim(orders, c, 1, False), C, T).reshape(-1)
    own_cos, own_sin = rotary_tables(own_places, 1.0)
    seq = c // R // HL
    seq_order = lax.dynamic_index_in_dim(orders, seq, 0, False)
    seq_cut = lax.dynamic_index_in_dim(cuts, seq, 0, False)
    tables = attention_tables(block_places(seq_order, C, T).reshape(-1), seq_cut)
    acts_own, own_cos, own_sin, *tables = lax.optimization_barrier((acts, own_cos, own_sin, *tables))
    blocks_down = with_other_core(own_down)
    acts_all = jnp.zeros((W, T, 2 * D), bf16)
    acts_all = lax.dynamic_update_slice_in_dim(acts_all, acts_own[None], z, 0)
    for k in range(1, W):
        if k == 2:
            acts_all, *blocks_down = lax.optimization_barrier((acts_all, *blocks_down))
        acts_all = lax.dynamic_update_slice_in_dim(acts_all, shift(acts, k)[None], (z - k) % W, 0)
    acts = acts_all.reshape(W * T, 2 * D)
    g = acts[:, D:]
    held, acts = lax.optimization_barrier((held, acts))
    pack = held[:, W * DL : W * DL + W, : 3 * E]
    pieces = [pack[:, :, s : s + n].astype(f32) for s, n in zip(starts, sizes)]
    bias_qkv, bias_dense, bias_up, bias_down, ga, sa, gm, sm = [p.reshape(-1) for p in pieces[:8]]
    bias_qkv = lax.dynamic_index_in_dim(bias_qkv.reshape(3, W, HL, HEAD_DIM), z, 1, False).transpose(1, 0, 2).reshape(3 * E)
    bias_up = lax.dynamic_index_in_dim(pieces[2], z, 1, False).reshape(C * FL)

    send, h_attn, full_dense = project(acts, ga, sa, held, bias_qkv, own_cos, own_sin, PART, T, c)
    send = send.reshape(PAIRS, T, 4 * HEAD_DIM)
    if R > 1:
        send = jnp.repeat(send, R, 0)
    packed = exchange(send, CTX).reshape(C * T, 4 * HEAD_DIM)

    h_mlp, hidden, d_pre, out_mlp, sum_pre = feed_forward(
        after(acts, send), gm, sm, held, bias_up, blocks_down, PART, c
    )
    result = attention(after(packed, d_pre), *tables)

    h_late = after(h_mlp, result)
    result = exchange(result.reshape(C, T, 4 * HEAD_DIM), CTX)
    away_up = hop(product_away(h_late, d_pre))
    own_down, other_down = product_by_core(after(hidden, away_up), acts, C, c)
    kept_up = product_plus(h_late, d_pre, away_up)
    result = after(result, own_down, kept_up)
    arrived_up = exchange(after(kept_up, result).reshape(C // 2, PART, C * FL), "chip")
    if R > 1:
        result = result.reshape(PAIRS, R, T, 4 * HEAD_DIM)[:, 0]
    attended, d_proj, sum_proj, away_qkv, out_part = unpack(
        result.reshape(W, HL, T, 4 * HEAD_DIM), h_attn, full_dense, out_mlp
    )
    away_here = hop(away_qkv)
    out_sum = lax.psum_scatter(out_part.reshape(W * T, D), "wsh", scatter_dimension=0, tiled=True)
    kept_qkv = product_plus(h_attn, d_proj, away_here)
    e_mlp, sums_mlp = input_terms(after(d_pre, kept_qkv), held, 4, acts, gm, PART)
    e_part, sums_attn = input_terms(d_proj, held, 0, acts, ga, PART, e_mlp)
    e_raw = e_part
    arrived_up = after(arrived_up, e_raw)
    arrived_qkv = exchange(after(kept_qkv, arrived_up).reshape(C // 2, PART, 3 * E), "chip")
    e_part, out_sum = lax.optimization_barrier((e_part, out_sum))
    e_sum = lax.psum_scatter(e_part, "wsh", scatter_dimension=0, tiled=True)

    gw_dense = t_dot(after(attended, arrived_up), g).astype(bf16).reshape(C // 2, 2, DL, D)
    kept_dense = over_cores_add(gw_dense, over_cores_send(gw_dense))
    kept_down = (after(own_down, e_raw).astype(f32) + hop(after(other_down, e_raw)).astype(f32)).astype(bf16)
    own_up = sum_arrived(arrived_up)
    arrived_qkv = after(arrived_qkv, own_up, kept_dense, kept_down)
    own_grads = jnp.concatenate([sum_arrived(arrived_qkv), own_up], 1)
    back = exchange(own_grads.reshape(W, DL, 7 * E), "wsh")
    grad_down = lax.psum_scatter(
        after(kept_down, arrived_qkv).reshape(C // 2 * FL, D), "chip", scatter_dimension=0, tiled=True
    ).astype(f32)
    terms = [lax.dynamic_index_in_dim(kept_dense, lax.axis_index("chip") ^ k, 0, False) for k in range(C // 2)]
    grad_dense = lax.ppermute(sum_terms(terms[0], hop_terms(terms)), both, back_moves).astype(f32)

    output = x + out_sum.astype(f32) + (bias_dense + bias_down)
    e = e_sum.astype(f32)
    input_gradient = (
        cot + (e - jnp.mean(e, -1, keepdims=True) - normed * jnp.mean(e * normed, -1, keepdims=True)) * inv_std
    )
    grad_qkv = join_qkv(back, 3 * E)
    grad_up = join_up(back, 3 * E, C)

    sum_proj = sum_proj.reshape(HL, 3, HEAD_DIM).transpose(1, 0, 2).reshape(3, 1, E)
    gb_qkv = lax.dynamic_update_slice_in_dim(jnp.zeros((3, W, E), f32), sum_proj, z, 1).reshape(C * W, -1)
    gb_up = lax.dynamic_update_slice_in_dim(jnp.zeros((C, W, FL), f32), sum_pre.reshape(C, 1, FL), z, 1)
    gb_up = gb_up.reshape(C * W, FL)
    by_width = jnp.concatenate([sums_attn, sums_mlp, jnp.sum(cot, 0, keepdims=True)], 0)
    by_width = by_width.reshape(5, C * W, DL).transpose(1, 0, 2).reshape(C * W, 5 * DL)
    vectors = jnp.concatenate([gb_up, gb_qkv, by_width], 1)
    summed = exchange(after(vectors, back), both)
    summed = jnp.sum(after(summed, grad_qkv, grad_up, input_gradient, output), 0)
    n_up, n_qkv = gb_up.shape[1], gb_qkv.shape[1]
    gb_up, gb_qkv = summed[:n_up], summed[n_up : n_up + n_qkv]
    g_ga, g_sa, g_gm, g_sm, gb_dense = [
        summed[n_up + n_qkv + i * DL : n_up + n_qkv + (i + 1) * DL] for i in range(5)
    ]
    return (
        output[None],
        input_gradient[None],
        grad_qkv,
        gb_qkv,
        grad_dense,
        gb_dense,
        grad_up,
        gb_up,
        grad_down,
        gb_dense,
        g_ga,
        g_sa,
        g_gm,
        g_sm,
    )


def solution(mesh):
    ctx, wsh = mesh.shape["ctx"], mesh.shape["wsh"]
    split = Mesh(mesh.devices.reshape(ctx // 2, 2, wsh), CTX + ("wsh",))
    tokens = P("wsh", CTX, None)
    matrix = P(CTX + ("wsh",), None)
    vector = P(CTX + ("wsh",))
    pairs = (matrix, vector) * 4
    return jax.shard_map(
        body,
        mesh=split,
        in_specs=(tokens, tokens, P("wsh", None), P("wsh")) + pairs + (vector,) * 4,
        out_specs=(tokens, tokens) + pairs + (vector,) * 4,
        check_vma=False,
    )
```

```python
import jax
import jax.numpy as jnp
from jax import lax
from jax.experimental import pallas as pl
from jax.experimental.pallas import tpu as pltpu
from jax.sharding import Mesh
from jax.sharding import PartitionSpec as P

HEADS = 8
HEAD_DIM = 256
ROT_DIM = 64
HALF = ROT_DIM // 2
NORM_EPS = 1e-05
LARGE_NEGATIVE = -1e30
SCALE = HEAD_DIM ** (-0.5)
f32 = jnp.float32
bf16 = jnp.bfloat16


def dot(a, b):
    return jnp.dot(a, b, preferred_element_type=f32)


def dot_t(a, b):
    return lax.dot_general(a, b, (((1,), (1,)), ((), ())), preferred_element_type=f32)


def t_dot(a, b):
    return lax.dot_general(a, b, (((0,), (0,)), ((), ())), preferred_element_type=f32)


def angles_of(places):
    frequency = jnp.power(10000.0, -2.0 * jnp.arange(HALF).astype(f32) / ROT_DIM)
    return places.astype(f32)[..., None] * frequency


def gelu_parts(pre_act):
    normal_cdf = 0.5 * (1.0 + lax.erf(pre_act * 0.7071067811865476))
    density = jnp.exp(-0.5 * pre_act * pre_act) * 0.3989422804014327
    return (pre_act * normal_cdf, normal_cdf + pre_act * density)


def block_places(order, ctx_count, tok_rows):
    half = tok_rows // 2
    within = jnp.arange(tok_rows, dtype=jnp.int32)
    first = order[..., None]
    block = jnp.where(within < half, first, 2 * ctx_count - 1 - first)
    return block * half + within % half


VMEM_LIMIT = 56 * 2**20


def rotary_tables(places, direction):
    angle = angles_of(places)
    cos, sin = jnp.cos(angle), jnp.sin(angle) * direction
    rest = 128 - ROT_DIM
    ones = jnp.ones((places.shape[0], rest), f32)
    return jnp.concatenate([cos, cos, ones], 1), jnp.concatenate([-sin, sin, 0.0 * ones], 1)


def turn(value, cos, sin):
    low = value[:, :128]
    lane = lax.broadcasted_iota(jnp.int32, low.shape, 1)
    other = jnp.where(lane < HALF, pltpu.roll(low, 128 - HALF, 1), pltpu.roll(low, HALF, 1))
    return jnp.concatenate([low * cos + other * sin, value[:, 128:]], 1)


class Columns:
    def __init__(self, array, unit, j):
        self.array, self.unit, self.j = array, unit, j
        self.shape = array.shape[:-1] + (unit,)
        self.dtype = array.dtype
        self.size = array.size // array.shape[-1] * unit


def columns(array, unit, first, last):
    return [Columns(array, unit, j) for j in range(first, last)]


def call(kernel, outs, operands, flops, scratch=(), scalar=None):
    in_specs, arrays = [], []
    if scalar is not None:
        in_specs.append(pl.BlockSpec(memory_space=pltpu.SMEM))
        arrays.append(scalar.reshape(1).astype(jnp.int32))
    for operand in operands:
        if isinstance(operand, Columns):
            lead = (0,) * (len(operand.shape) - 1)
            in_specs.append(pl.BlockSpec(operand.shape, lambda i, lead=lead, j=operand.j: lead + (j,)))
            arrays.append(operand.array)
        else:
            zero = (0,) * len(operand.shape)
            in_specs.append(pl.BlockSpec(operand.shape, lambda i, zero=zero: zero))
            arrays.append(operand)
    out_specs = [pl.BlockSpec(o.shape, lambda i, zero=(0,) * len(o.shape): zero) for o in outs]
    return pl.pallas_call(
        kernel,
        grid=(1,),
        out_shape=outs,
        in_specs=in_specs,
        out_specs=out_specs,
        scratch_shapes=list(scratch),
        compiler_params=pltpu.CompilerParams(vmem_limit_bytes=VMEM_LIMIT),
        cost_estimate=pl.CostEstimate(flops=0, bytes_accessed=0, transcendentals=0),
    )(*arrays)


def kept_block(p, count, core):
    half = count // 2
    return 2 * (p % half) + (core if p < half else 1 - core)


def kept_difference(p, count):
    half = count // 2
    return 2 * (p % half) + p // half


def at(index, size):
    return pl.ds(pl.multiple_of(index * size, size), size)


def shaped(shape, dtype):
    return jax.ShapeDtypeStruct(shape, dtype)


def attention_kernel(x_ref, row_ref, key_ref, cos_ref, sin_ref, out_ref, dk_ref, dv_ref):
    length = x_ref.shape[0]
    hd = HEAD_DIM
    tile = min(256, length)
    keys = x_ref[:, hd : 2 * hd]
    values = x_ref[:, 2 * hd : 3 * hd]
    key_place = key_ref[0:1, :]
    for step in range(length // tile):
        rows = slice(step * tile, (step + 1) * tile)
        query = x_ref[rows, 0:hd]
        grad = x_ref[rows, 3 * hd : 4 * hd]
        place = row_ref[rows, 0:1]
        first = row_ref[rows, 1:2]
        allowed = (key_place <= place) & (key_place >= first)
        scores = jnp.where(allowed, dot_t(query, keys) * SCALE, LARGE_NEGATIVE)
        top = jnp.max(scores, 1, keepdims=True)
        weights = jnp.exp(scores - top)
        probs = weights * (1.0 / jnp.sum(weights, 1, keepdims=True))
        probs_b = probs.astype(bf16)
        attended = dot(probs_b, values).astype(bf16)
        out_ref[rows, 0:hd] = attended
        delta = jnp.sum(grad.astype(f32) * attended.astype(f32), 1, keepdims=True)
        d_probs = dot_t(grad, values)
        d_scores = (probs * (d_probs - delta) * SCALE).astype(bf16)
        d_query = dot(d_scores, keys)
        out_ref[rows, hd : 2 * hd] = turn(d_query, cos_ref[rows, :], sin_ref[rows, :]).astype(bf16)
        dk = t_dot(d_scores, query)
        dv = t_dot(probs_b, grad)
        if step == 0:
            dk_ref[...] = dk
            dv_ref[...] = dv
        else:
            dk_ref[...] += dk
            dv_ref[...] += dv
    for step in range(length // tile):
        rows = slice(step * tile, (step + 1) * tile)
        out_ref[rows, 2 * hd : 3 * hd] = turn(dk_ref[rows, :], cos_ref[rows, :], sin_ref[rows, :]).astype(bf16)
        out_ref[rows, 3 * hd : 4 * hd] = dv_ref[rows, :].astype(bf16)


def attention_tables(places, cut):
    cos_table, sin_table = rotary_tables(places, -1.0)
    return jnp.stack([places, jnp.where(places >= cut, cut, 0)], 1), places[None, :], cos_table, sin_table


def attention(packed, *tables):
    length = packed.shape[0]
    scratch = [pltpu.VMEM((length, HEAD_DIM), f32), pltpu.VMEM((length, HEAD_DIM), f32)]
    outs = [shaped((length, 4 * HEAD_DIM), bf16)]
    return call(attention_kernel, outs, (packed, *tables), 12 * length * length * HEAD_DIM, scratch)[0]


def project(acts, gain, shift_by, held, bias, cos, sin, part, tokens, index):
    rows, width = acts.shape[0], acts.shape[1] // 2
    count, unit = held.shape[0], held.shape[2] // 8
    seqs = rows // tokens
    hd = HEAD_DIM
    heads = unit // hd
    pieces = width // unit
    size = part // pieces

    def kernel(*refs):
        index_ref, acts_ref, gain_ref, shift_ref, bias_ref, cos_ref, sin_ref = refs[:7]
        w_refs, dense_in_ref = refs[7:10], refs[10]
        send_ref, h_ref, dense_ref = refs[11:]
        core = index_ref[0] & 1
        for p in range(count):
            for j in range(pieces):
                block = dense_in_ref[p, j * size : (j + 1) * size, :]
                dense_ref[p * size : (p + 1) * size, j * unit : (j + 1) * unit] = block
            cols = at(kept_block(p, count, core), part)
            h = acts_ref[:, cols].astype(f32) * gain_ref[0:1, cols] + shift_ref[0:1, cols]
            h_ref[:, p * part : (p + 1) * part] = h.astype(bf16)
        for head in range(heads):
            for piece in range(3):
                start = (head * 3 + piece) * hd
                total = jnp.broadcast_to(bias_ref[0:1, start : start + hd], (rows, hd))
                w_ref, start = w_refs[start // unit], start % unit
                for p in range(count):
                    block = w_ref[kept_block(p, count, core), :part, start : start + hd]
                    total = total + dot(h_ref[:, p * part : (p + 1) * part], block)
                if piece < 2:
                    total = turn(total, cos_ref[...], sin_ref[...])
                send_ref[:, head, :, piece * hd : (piece + 1) * hd] = total.astype(bf16).reshape(seqs, tokens, hd)
            d_att = dot_t(acts_ref[:, width:], dense_ref[head * hd : (head + 1) * hd, :])
            send_ref[:, head, :, 3 * hd :] = d_att.astype(bf16).reshape(seqs, tokens, hd)

    outs = [
        shaped((seqs, heads, tokens, 4 * hd), bf16),
        shaped((rows, width), bf16),
        shaped((unit, width), bf16),
    ]
    operands = [acts, gain[None], shift_by[None], bias[None], cos, sin]
    operands += columns(held, unit, 0, 4)
    return call(kernel, outs, operands, 8 * rows * width * unit, scalar=index)


def feed_forward(acts, gain, shift_by, held, bias, down_blocks, part, index):
    rows, width = acts.shape[0], acts.shape[1] // 2
    count, unit = held.shape[0], held.shape[2] // 8
    size = down_blocks[0].shape[0]
    hidden_n = 4 * unit
    tile = 256

    def kernel(*refs):
        index_ref, acts_ref, gain_ref, shift_ref, bias_ref = refs[:5]
        up_refs = refs[5:9]
        down_refs = refs[9 : 9 + count]
        h_ref, hidden_ref, d_pre_ref, out_ref, sum_ref, down_ref = refs[9 + count :]
        core = index_ref[0] & 1
        for p in range(count):
            down_ref[at(index_ref[0] ^ kept_difference(p, count), size), :] = down_refs[p][...]
            cols = at(kept_block(p, count, core), part)
            h = acts_ref[:, cols].astype(f32) * gain_ref[0:1, cols] + shift_ref[0:1, cols]
            h_ref[:, p * part : (p + 1) * part] = h.astype(bf16)
        for step in range(hidden_n // tile):
            cols = slice(step * tile, (step + 1) * tile)
            up_ref, start = up_refs[step * tile // unit], step * tile % unit
            pre = jnp.broadcast_to(bias_ref[0:1, cols], (rows, tile))
            for p in range(count):
                block = up_ref[kept_block(p, count, core), :part, start : start + tile]
                pre = pre + dot(h_ref[:, p * part : (p + 1) * part], block)
            activated, slope = gelu_parts(pre)
            hidden_ref[:, cols] = activated.astype(bf16)
            d_pre = dot_t(acts_ref[:, width:], down_ref[cols, :]) * slope
            sum_ref[0:1, cols] = jnp.sum(d_pre, 0, keepdims=True)
            d_pre_ref[:, cols] = d_pre.astype(bf16)
        for step in range(width // 256):
            cols = slice(step * 256, (step + 1) * 256)
            out_ref[:, cols] = dot(hidden_ref[...], down_ref[:, cols])

    outs = [
        shaped((rows, width), bf16),
        shaped((rows, hidden_n), bf16),
        shaped((rows, hidden_n), bf16),
        shaped((rows, width), f32),
        shaped((1, hidden_n), f32),
    ]
    operands = [acts, gain[None], shift_by[None], bias[None]] + columns(held, unit, 4, 8) + list(down_blocks)
    scratch = [pltpu.VMEM((hidden_n, width), bf16)]
    return call(kernel, outs, operands, 6 * rows * width * hidden_n, scratch, scalar=index)


def input_terms(d_out, held, first, acts, gain, part, e_before=None):
    rows, width = acts.shape[0], acts.shape[1] // 2
    count, unit = held.shape[0], held.shape[2] // 8
    units = d_out.shape[1] // unit

    def kernel(*refs):
        d_out_ref, acts_ref, gain_ref = refs[:3]
        w_refs = refs[3 : 3 + units]
        e_ref, sum_ref = refs[-2:]
        for p in range(count):
            cols = slice(p * part, (p + 1) * part)
            d_h = dot_t(d_out_ref[:, :unit], w_refs[0][p, :part, :])
            for j in range(1, units):
                d_h = d_h + dot_t(d_out_ref[:, j * unit : (j + 1) * unit], w_refs[j][p, :part, :])
            sum_ref[0:1, cols] = jnp.sum(d_h * acts_ref[:, cols].astype(f32), 0, keepdims=True)
            sum_ref[1:2, cols] = jnp.sum(d_h, 0, keepdims=True)
            e = d_h * gain_ref[0:1, cols]
            if e_before is not None:
                e = e + refs[3 + units][:, cols]
            e_ref[:, cols] = e.astype(e_ref.dtype)

    outs = [shaped((rows, width), f32 if e_before is None else bf16), shaped((2, width), f32)]
    operands = [d_out, acts, gain[None]] + columns(held, unit, first, first + units)
    if e_before is not None:
        operands.append(e_before)
    return call(kernel, outs, operands, 2 * rows * width * d_out.shape[1])


def split_columns(w_qkv, w_up, wsh, ctx):
    rows = w_qkv.shape[0]
    width = w_qkv.shape[1] // 3
    hd = HEAD_DIM
    heads = HEADS // wsh
    fl = w_up.shape[1] // (ctx * wsh)

    def kernel(qkv_ref, up_ref, out_ref):
        for z in range(wsh):
            for head in range(heads):
                for piece in range(3):
                    start = piece * width + (z * heads + head) * hd
                    to = (head * 3 + piece) * hd
                    out_ref[z, :, to : to + hd] = qkv_ref[:, start : start + hd]
            out_ref[z, :, 3 * heads * hd :] = jnp.concatenate(
                [up_ref[:, (c * wsh + z) * fl : (c * wsh + z + 1) * fl] for c in range(ctx)], 1
            )

    outs = [shaped((wsh, rows, 3 * heads * hd + ctx * fl), bf16)]
    return call(kernel, outs, (w_qkv, w_up), 0)[0]


def join_qkv(parts, columns):
    wsh, rows, _ = parts.shape
    hd = HEAD_DIM
    heads = HEADS // wsh

    def kernel(in_ref, out_ref):
        for z in range(wsh):
            for head in range(heads):
                for piece in range(3):
                    to = piece * HEADS * hd + (z * heads + head) * hd
                    start = (head * 3 + piece) * hd
                    out_ref[:, to : to + hd] = in_ref[z, :, start : start + hd].astype(f32)

    return call(kernel, [shaped((rows, wsh * columns), f32)], (parts,), 0)[0]


def join_up(parts, first, ctx):
    wsh, rows, columns = parts.shape
    fl = (columns - first) // ctx

    def kernel(in_ref, out_ref):
        for c in range(ctx):
            start = first + c * fl
            out_ref[:, c * wsh * fl : (c + 1) * wsh * fl] = jnp.concatenate(
                [in_ref[z, :, start : start + fl].astype(f32) for z in range(wsh)], 1
            )

    return call(kernel, [shaped((rows, wsh * (columns - first)), f32)], (parts,), 0)[0]


def unpack(result, h_kept, dense, out_mlp):
    seqs, heads, tokens, _ = result.shape
    hd = HEAD_DIM
    rows, width = out_mlp.shape
    half = width // 2
    tile = 256

    def kernel(in_ref, h_ref, dense_ref, out_mlp_ref, att_ref, proj_ref, sum_ref, away_ref, out_ref):
        for head in range(heads):
            value = in_ref[:, head].reshape(rows, 4 * hd)
            att_ref[:, head * hd : (head + 1) * hd] = value[:, :hd]
            proj_ref[:, head * 3 * hd : (head + 1) * 3 * hd] = value[:, hd:]
            sum_ref[0:1, head * 3 * hd : (head + 1) * 3 * hd] = jnp.sum(value[:, hd:].astype(f32), 0, keepdims=True)
        for start in range(0, half, tile):
            away_ref[start : start + tile, :] = t_dot(h_ref[:, half + start : half + start + tile], proj_ref[...]).astype(bf16)
        for start in range(0, width, tile):
            cols = slice(start, start + tile)
            out_ref[:, cols] = (out_mlp_ref[:, cols] + dot(att_ref[...], dense_ref[:, cols])).astype(bf16)

    outs = [
        shaped((rows, heads * hd), bf16),
        shaped((rows, heads * 3 * hd), bf16),
        shaped((1, heads * 3 * hd), f32),
        shaped((half, heads * 3 * hd), bf16),
        shaped((rows, width), bf16),
    ]
    return call(kernel, outs, (result, h_kept, dense, out_mlp), 0)


def product_plus(left, right, term):
    tile = 256

    def kernel(left_ref, right_ref, term_ref, out_ref):
        for start in range(0, left.shape[1] // 2, tile):
            rows = slice(start, start + tile)
            out_ref[rows, :] = (t_dot(left_ref[:, rows], right_ref[...]) + term_ref[rows, :].astype(f32)).astype(bf16)

    return call(kernel, [shaped(term.shape, bf16)], (left, right, term), 0)[0]


def product_by_core(left, acts, count, index):
    width = acts.shape[1] // 2
    size = left.shape[1] // count

    def kernel(index_ref, left_ref, acts_ref, own_ref, other_ref):
        core = index_ref[0] & 1
        for j in range(count // 2):
            for o in range(2):
                start = (2 * j + o) * size
                value = t_dot(left_ref[:, start : start + size], acts_ref[:, width:]).astype(bf16)

                @pl.when(core == o)
                def _():
                    own_ref[j] = value

                @pl.when(core != o)
                def _():
                    other_ref[j] = value

    outs = [shaped((count // 2, size, width), bf16)] * 2
    return call(kernel, outs, (left, acts), 0, scalar=index)


CTX = ("chip", "core")


def after(value, *others):
    return lax.optimization_barrier((value,) + others)[0]


def hop(value):
    return lax.ppermute(value, "core", [(0, 1), (1, 0)])


def exchange(value, axis):
    return lax.all_to_all(value, axis, 0, 0, tiled=True)


def chip_hop(value, k):
    n = lax.axis_size("chip")
    return lax.ppermute(value, "chip", [(i, i ^ k) for i in range(n)])


def shift(value, step):
    n = lax.axis_size("wsh")
    return lax.ppermute(value, "wsh", [(i, (i + step) % n) for i in range(n)])


def chip_blocks(block):
    return [block] + [chip_hop(block, k) for k in range(1, lax.axis_size("chip"))]


def with_other_core(own):
    return list(own) + [hop(value) for value in own]


def sum_arrived(value):
    return jnp.sum(value.astype(f32), 0).astype(bf16)


def over_cores_send(value):
    return hop(lax.dynamic_index_in_dim(value, 1 - lax.axis_index("core"), 1, False))


def over_cores_add(value, away):
    kept = lax.dynamic_index_in_dim(value, lax.axis_index("core"), 1, False)
    return (kept.astype(f32) + away.astype(f32)).astype(bf16)


def hop_terms(terms):
    return [chip_hop(term, k) for k, term in enumerate(terms) if k]


def sum_terms(own, arrived):
    total = own.astype(f32)
    for term in arrived:
        total = total + term.astype(f32)
    return total.astype(bf16)


def body(
    inputs,
    cotangent,
    block_order,
    doc_cut,
    w_qkv,
    b_qkv,
    w_dense,
    b_dense,
    w_up,
    b_up,
    w_down,
    b_down,
    gain_attn,
    shift_attn,
    gain_mlp,
    shift_mlp,
):
    both = CTX + ("wsh",)
    C = lax.axis_size(CTX)
    W = lax.axis_size("wsh")
    core = lax.axis_index("core")
    c = lax.axis_index(CTX)
    z = lax.axis_index("wsh")
    T, D = inputs.shape[1:]
    DL = w_qkv.shape[0]
    FL = w_down.shape[0]
    E = D // W
    HL = HEADS // W
    PAIRS = W * HL
    R = C // PAIRS
    PART = D // C
    x = inputs[0]
    cot = cotangent[0]

    moves = [(i, (i % C) * W + i // C) for i in range(C * W)]
    back_moves = [(j, i) for i, j in moves]
    own_down = chip_blocks(w_down)
    moved_dense = lax.ppermute(w_dense, both, moves)

    centre = x - jnp.mean(x, -1, keepdims=True)
    inv_std = lax.rsqrt(jnp.mean(centre * centre, -1, keepdims=True) + NORM_EPS)
    normed = centre * inv_std
    acts = jnp.concatenate([normed.astype(bf16), cot.astype(bf16)], 1)
    cut = doc_cut[0]
    ints = jnp.concatenate([block_order[0], (cut // 16)[None], (cut % 16)[None]]).astype(bf16)
    small = [b_qkv, b_dense, b_up, b_down, gain_attn, shift_attn, gain_mlp, shift_mlp, ints]
    sizes = [a.shape[0] for a in small]
    starts = [sum(sizes[:i]) for i in range(len(sizes))]
    rider = jnp.concatenate(small + [jnp.zeros((3 * E - sum(sizes),), bf16)])
    turned = exchange(split_columns(w_qkv, w_up, W, C), "wsh")
    rider = jnp.broadcast_to(rider, (16, 3 * E))
    riders = jnp.broadcast_to(rider[:1], (16, 3 * E))
    for k in range(1, W):
        riders = lax.dynamic_update_slice_in_dim(riders, shift(rider, k)[:1], (z - k) % W, 0)
    riders = lax.dynamic_update_slice_in_dim(riders, rider[:1], z, 0)
    turned, acts, riders, moved_dense, *own_down = lax.optimization_barrier((turned, acts, riders, moved_dense, *own_down))
    dense_part = moved_dense.reshape(DL, W, E).transpose(1, 0, 2).reshape(W * DL, E)
    turned = turned.reshape(W * DL, 7 * E)
    held = jnp.concatenate([turned[:, : 3 * E], dense_part, turned[:, 3 * E :]], 1)
    held = jnp.concatenate([held, jnp.pad(riders, ((0, 0), (0, 5 * E)))], 0)
    held = lax.all_gather(held[None], CTX, axis=0, tiled=True)
    info = riders[:W, starts[-1] : starts[-1] + sizes[-1]].astype(f32).astype(jnp.int32)
    orders = info[:, :C]
    cuts = info[:, C] * 16 + info[:, C + 1]
    own_places = block_places(lax.dynamic_index_in_dim(orders, c, 1, False), C, T).reshape(-1)
    own_cos, own_sin = rotary_tables(own_places, 1.0)
    seq = c // R // HL
    seq_order = lax.dynamic_index_in_dim(orders, seq, 0, False)
    seq_cut = lax.dynamic_index_in_dim(cuts, seq, 0, False)
    tables = attention_tables(block_places(seq_order, C, T).reshape(-1), seq_cut)
    acts_own, own_cos, own_sin, *tables = lax.optimization_barrier((acts, own_cos, own_sin, *tables))
    blocks_down = with_other_core(own_down)
    acts_all = jnp.zeros((W, T, 2 * D), bf16)
    acts_all = lax.dynamic_update_slice_in_dim(acts_all, acts_own[None], z, 0)
    for k in range(1, W):
        if k == 2:
            acts_all, *blocks_down = lax.optimization_barrier((acts_all, *blocks_down))
        acts_all = lax.dynamic_update_slice_in_dim(acts_all, shift(acts, k)[None], (z - k) % W, 0)
    acts = acts_all.reshape(W * T, 2 * D)
    g = acts[:, D:]
    held, acts = lax.optimization_barrier((held, acts))
    pack = held[:, W * DL : W * DL + W, : 3 * E]
    pieces = [pack[:, :, s : s + n].astype(f32) for s, n in zip(starts, sizes)]
    bias_qkv, bias_dense, bias_up, bias_down, ga, sa, gm, sm = [p.reshape(-1) for p in pieces[:8]]
    bias_qkv = lax.dynamic_index_in_dim(bias_qkv.reshape(3, W, HL, HEAD_DIM), z, 1, False).transpose(1, 0, 2).reshape(3 * E)
    bias_up = lax.dynamic_index_in_dim(pieces[2], z, 1, False).reshape(C * FL)

    send, h_attn, full_dense = project(acts, ga, sa, held, bias_qkv, own_cos, own_sin, PART, T, c)
    send = send.reshape(PAIRS, T, 4 * HEAD_DIM)
    if R > 1:
        send = jnp.repeat(send, R, 0)
    packed = exchange(send, CTX).reshape(C * T, 4 * HEAD_DIM)

    h_mlp, hidden, d_pre, out_mlp, sum_pre = feed_forward(
        after(acts, send), gm, sm, held, bias_up, blocks_down, PART, c
    )
    result = attention(after(packed, d_pre), *tables)

    h_late = after(h_mlp, result)
    result = exchange(result.reshape(C, T, 4 * HEAD_DIM), CTX)
    away_up = hop(t_dot(h_late[:, D // 2 :], d_pre).astype(bf16))
    own_down, other_down = product_by_core(after(hidden, away_up), acts, C, c)
    kept_up = product_plus(h_late, d_pre, away_up)
    result = after(result, own_down, kept_up)
    arrived_up = exchange(after(kept_up, result).reshape(C // 2, PART, C * FL), "chip")
    if R > 1:
        result = result.reshape(PAIRS, R, T, 4 * HEAD_DIM)[:, 0]
    attended, d_proj, sum_proj, away_qkv, out_part = unpack(
        result.reshape(W, HL, T, 4 * HEAD_DIM), h_attn, full_dense, out_mlp
    )
    away_here = hop(away_qkv)
    out_sum = lax.psum_scatter(out_part.reshape(W * T, D), "wsh", scatter_dimension=0, tiled=True)
    kept_qkv = product_plus(h_attn, d_proj, away_here)
    e_mlp, sums_mlp = input_terms(after(d_pre, kept_qkv), held, 4, acts, gm, PART)
    e_part, sums_attn = input_terms(d_proj, held, 0, acts, ga, PART, e_mlp)
    e_raw = e_part
    arrived_up = after(arrived_up, e_raw)
    arrived_qkv = exchange(after(kept_qkv, arrived_up).reshape(C // 2, PART, 3 * E), "chip")
    e_part, out_sum = lax.optimization_barrier((e_part, out_sum))
    e_sum = lax.psum_scatter(e_part, "wsh", scatter_dimension=0, tiled=True)

    gw_dense = t_dot(after(attended, arrived_up), g).astype(bf16).reshape(C // 2, 2, DL, D)
    kept_dense = over_cores_add(gw_dense, over_cores_send(gw_dense))
    kept_down = (after(own_down, e_raw).astype(f32) + hop(after(other_down, e_raw)).astype(f32)).astype(bf16)
    own_up = sum_arrived(arrived_up)
    arrived_qkv = after(arrived_qkv, own_up, kept_dense, kept_down)
    own_grads = jnp.concatenate([sum_arrived(arrived_qkv), own_up], 1)
    back = exchange(own_grads.reshape(W, DL, 7 * E), "wsh")
    grad_down = lax.psum_scatter(
        after(kept_down, arrived_qkv).reshape(C // 2 * FL, D), "chip", scatter_dimension=0, tiled=True
    ).astype(f32)
    terms = [lax.dynamic_index_in_dim(kept_dense, lax.axis_index("chip") ^ k, 0, False) for k in range(C // 2)]
    grad_dense = lax.ppermute(sum_terms(terms[0], hop_terms(terms)), both, back_moves).astype(f32)

    output = x + out_sum.astype(f32) + (bias_dense + bias_down)
    e = e_sum.astype(f32)
    input_gradient = (
        cot + (e - jnp.mean(e, -1, keepdims=True) - normed * jnp.mean(e * normed, -1, keepdims=True)) * inv_std
    )
    grad_qkv = join_qkv(back, 3 * E)
    grad_up = join_up(back, 3 * E, C)

    sum_proj = sum_proj.reshape(HL, 3, HEAD_DIM).transpose(1, 0, 2).reshape(3, 1, E)
    gb_qkv = lax.dynamic_update_slice_in_dim(jnp.zeros((3, W, E), f32), sum_proj, z, 1).reshape(C * W, -1)
    gb_up = lax.dynamic_update_slice_in_dim(jnp.zeros((C, W, FL), f32), sum_pre.reshape(C, 1, FL), z, 1)
    gb_up = gb_up.reshape(C * W, FL)
    by_width = jnp.concatenate([sums_attn, sums_mlp, jnp.sum(cot, 0, keepdims=True)], 0)
    by_width = by_width.reshape(5, C * W, DL).transpose(1, 0, 2).reshape(C * W, 5 * DL)
    vectors = jnp.concatenate([gb_up, gb_qkv, by_width], 1)
    summed = exchange(after(vectors, grad_qkv, grad_up, input_gradient, output), both)
    summed = jnp.sum(after(summed, grad_down, grad_dense), 0)
    n_up, n_qkv = gb_up.shape[1], gb_qkv.shape[1]
    gb_up, gb_qkv = summed[:n_up], summed[n_up : n_up + n_qkv]
    g_ga, g_sa, g_gm, g_sm, gb_dense = [
        summed[n_up + n_qkv + i * DL : n_up + n_qkv + (i + 1) * DL] for i in range(5)
    ]
    return (
        output[None],
        input_gradient[None],
        grad_qkv,
        gb_qkv,
        grad_dense,
        gb_dense,
        grad_up,
        gb_up,
        grad_down,
        gb_dense,
        g_ga,
        g_sa,
        g_gm,
        g_sm,
    )


def solution(mesh):
    ctx, wsh = mesh.shape["ctx"], mesh.shape["wsh"]
    split = Mesh(mesh.devices.reshape(ctx // 2, 2, wsh), CTX + ("wsh",))
    tokens = P("wsh", CTX, None)
    matrix = P(CTX + ("wsh",), None)
    vector = P(CTX + ("wsh",))
    pairs = (matrix, vector) * 4
    return jax.shard_map(
        body,
        mesh=split,
        in_specs=(tokens, tokens, P("wsh", None), P("wsh")) + pairs + (vector,) * 4,
        out_specs=(tokens, tokens) + pairs + (vector,) * 4,
        check_vma=False,
    )
```
